32 devices in a mesh: groups: 2 (over x), tile: 8 (over z, y), pos: 2 (over core).
Axes of the slice: x: 2, y: 2, z: 4, core: 2. Of those that a mesh axis runs over, the one named last changes fastest.
Arguments:
- object_field: float32 [4, 4096, 1024], P('groups', 'tile'), parts along dimension 0, may hold values from -6 to 6
- probe: float32 [8, 2, 128, 128], P('groups'), parts along dimension 0, may hold values from -3 to 3
- patterns: bfloat16 [1024, 128, 128], P(('groups', 'tile', 'pos')), parts along dimension 0, may hold values from 0.5 to 3.5
- scan_tile: int32 [1024, 1], P(('groups', 'tile', 'pos')), parts along dimension 0, may hold values from 0 to 7; in each aligned block of 32 rows (0 to 31, 32 to 63, ...) at most 8 rows name the same one
- scan_row: int32 [1024], P(('groups', 'tile', 'pos')), parts along dimension 0, may hold values from 0 to 384
- scan_col: int32 [1024], P(('groups', 'tile', 'pos')), parts along dimension 0, may hold values from 0 to 896
Outputs:
- object_step: float32 [4, 4096, 1024], P('groups', 'tile', 'pos'), parts along dimension 0
- probe_step: float32 [8, 2, 128, 128], P('groups'), parts along dimension 0
The draws below stay inside these ranges and needn't reach their ends.
There are 2 independent parts, one for each index of `groups`. The reference program is written for one: setup_inputs(seed, part) draws one part's arguments, and reference() takes and returns one part's arrays. A program takes and returns all parts, laid end to end along the dimension named above; each array names one. Nothing has to cross between parts.
Inputs may be any that keep to these rules, and one draw needn't show every extreme that they name: `scan_tile`: among the 32 positions of one device at most 8 lie in one tile, and some device has exactly 8 in some tile.
All inputs are finite; a program needn't handle non-finite values.
Results may differ from the reference program's by a relative error of at most 0.0035.
The reference program's roundings to bfloat16 on the way count: a program that leaves them out, or rounds other values in their place, can miss the bound.
Values may be sent and summed in bfloat16 or wider, within the bound.
No kernel may reach another device: no remote copies, remote signals or barrier semaphores. Data moves between devices by JAX's collectives and lax.ppermute only.
A program may use at most 64 MiB of HBM per device.

```python
import math
import jax
import jax.numpy as jnp
import numpy as np
from jax import lax

PATCH = 128
MODES = 4
SCAN_DEV = 32
TILE_R = 512
OBJ_C = 1024
CAP = 8
SCANS = 512
OBJ_R = 4096
N_TILE = 8


def with_ends(array, rng, smallest, high):
    longest = array.shape.index(max(array.shape))
    spots = []
    for shift in (0, 1):
        where = [jax.random.randint(jax.random.fold_in(rng, axis), (), 0, length) for axis, length in enumerate(array.shape)]
        where[longest] = (where[longest] + shift) % array.shape[longest]
        spots.append(tuple(where))
    return array.at[spots[0]].set(smallest).at[spots[1]].set(high)


def block_levels(rng, shape, pieces, least, high):
    level = 1.0
    for axis_at, blocks in pieces:
        steps = jax.random.uniform(jax.random.fold_in(jax.random.fold_in(rng, 6), axis_at), (blocks,), jnp.float32, least / len(pieces), high / len(pieces))
        level = level * jnp.repeat(jnp.exp(steps), shape[axis_at] // blocks).reshape((-1,) + (1,) * (len(shape) - 1 - axis_at))
    return level


def deal_out(stream_key, own, number, rows, number_of, top, most, lean):
    ranking = jax.random.permutation(stream_key, number_of)
    crowded, usual = portions_of(number_of, rows * top, most, lean, True), portions_of(number_of, rows * top, most, lean, False)
    places = jnp.arange(number_of)

    def named(lengths, turn):
        used = int((lengths > 0).sum())
        fixed = max(1, used // 4)
        moved = fixed + (places - fixed + turn * (used - fixed)) % max(1, number_of - fixed)
        return jnp.zeros((number_of,), jnp.int32).at[ranking[jnp.where(places < fixed, places, moved)]].set(jnp.asarray(lengths, jnp.int32))

    lengths = jnp.where(number % 4 == 0, named(crowded, number // 4), named(usual, number - number // 4 - 1))
    mixed = jax.random.permutation(jax.random.fold_in(own, 3), number_of)
    source_of, receiver = mixed[0:number_of // 2 * 2:2], mixed[1:number_of // 2 * 2:2]
    margin = jnp.minimum(lengths[source_of] - 1, most - lengths[receiver]) // 2
    margin = jnp.where((source_of == ranking[0]) | (receiver == ranking[0]) | (lengths[receiver] == 0), 0, jnp.maximum(margin, 0))
    moved = jax.random.randint(jax.random.fold_in(own, 4), (number_of // 2,), 0, 1 << 20) % (margin + 1)
    lengths = lengths.at[source_of].add(-moved).at[receiver].add(moved)
    labels = jnp.searchsorted(jnp.cumsum(lengths), jnp.arange(rows * top), side="right").astype(jnp.int32)
    listing = labels.reshape(top, rows).T
    listing = listing[jax.random.permutation(jax.random.fold_in(own, 1), rows)]
    turn = jax.random.randint(jax.random.fold_in(own, 2), (rows, 1), 0, top)
    return jnp.take_along_axis(listing, (jnp.arange(top)[None, :] + turn) % top, axis=1)


def portions_of(count, total, reach, lean, full):
    loads = [(1 << 20) // math.isqrt(rank ** lean) + 1 for rank in range(1, count + 1)]
    largest = reach if full else min(reach, max(-(-total // count), total * loads[0] // sum(loads)))
    least = 1 if total - largest >= count - 1 else 0
    holding, rest = [largest] + [least] * (count - 1), total - largest - least * (count - 1)
    while rest > 0:
        candidates = [i for i in range(1, count) if holding[i] < largest] or [i for i in range(1, count) if holding[i] < reach]
        pool, remaining = sum([loads[i] for i in candidates]), rest
        for i in candidates:
            extra = min(reach - holding[i], max(1, remaining * loads[i] // pool), rest)
            holding[i] = holding[i] + extra
            rest = rest - extra
    return np.array(holding)


def normal_values(rng, extent, spread, limit, shards=(), held_as=jnp.bfloat16):
    loudness = block_levels(rng, extent, shards, -0.22, 0.18) if shards else 1.0
    array = jax.random.normal(rng, extent, jnp.float32) * spread * loudness
    return jnp.minimum(jnp.maximum(array, -limit), limit).astype(held_as)


def setup_inputs(seed: int = 0, part: int = 0) -> dict:
    splits = jax.random.split(jax.random.key(seed), 7)
    own_keys = jax.random.split(jax.random.fold_in(splits[6], part), 7)
    object_field = normal_values(own_keys[0], (2, OBJ_R, OBJ_C), 1.0, 6.0, ((1, 8),), jnp.float32)
    probe = normal_values(own_keys[1], (MODES, 2, PATCH, PATCH), 0.5, 3.0, (), jnp.float32)
    patterns = jnp.clip(0.5 + 3.0 * jax.random.uniform(own_keys[2], (SCANS, PATCH, PATCH), jnp.float32) ** block_levels(own_keys[2], (SCANS, PATCH, PATCH), ((0, 16),), -0.2, 0.2), 0.5, 3.5).astype(jnp.bfloat16)
    scan_tile_keys = jax.random.split(jax.random.fold_in(own_keys[3], 1), SCANS // SCAN_DEV)
    scan_tile_turns = jax.random.permutation(jax.random.fold_in(own_keys[3], 3), SCANS // SCAN_DEV)
    scan_tile = jax.vmap(lambda own, number: deal_out(jax.random.fold_in(own_keys[3], 2), own, number, SCAN_DEV, N_TILE, 1, CAP, 2))(scan_tile_keys, scan_tile_turns).reshape((SCANS, 1))
    scan_row = with_ends(jax.random.randint(own_keys[4], (SCANS,), 0, TILE_R - PATCH + 1), jax.random.fold_in(own_keys[4], 1), 0, TILE_R - PATCH).astype(jnp.int32)
    scan_col = with_ends(jax.random.randint(own_keys[5], (SCANS,), 0, OBJ_C - PATCH + 1), jax.random.fold_in(own_keys[5], 1), 0, OBJ_C - PATCH).astype(jnp.int32)
    return dict(object_field=object_field, probe=probe, patterns=patterns, scan_tile=scan_tile, scan_row=scan_row, scan_col=scan_col)


AMP_FLOOR = 0.5

def dft_parts(length):
    indices = jnp.arange(length, dtype=jnp.int32)
    products = indices[:, None] * indices[None, :] % length
    angles = products.astype(jnp.float32) * (-2.0 * math.pi / length)
    factor = 1.0 / math.sqrt(length)
    return (jnp.cos(angles) * factor, jnp.sin(angles) * factor)

def chirp_parts(length):
    offsets = jnp.arange(length, dtype=jnp.int32) - length // 2
    squares = offsets * offsets
    phases = (squares[:, None] + squares[None, :]).astype(jnp.float32) * (0.5 * math.pi / length)
    return (jnp.cos(phases), jnp.sin(phases))

def left_matrix(real_part, imag_part):
    upper = jnp.concatenate([real_part, -imag_part], 1)
    lower = jnp.concatenate([imag_part, real_part], 1)
    return jnp.concatenate([upper, lower], 0)

def right_matrix(real_part, imag_part):
    return jnp.concatenate([real_part, imag_part], 1)

def make_tables(length):
    dft_real, dft_imag = dft_parts(length)
    dft_real = dft_real.astype(jnp.bfloat16)
    dft_imag = dft_imag.astype(jnp.bfloat16)
    chirp_real, chirp_imag = chirp_parts(length)
    return (left_matrix(dft_real, dft_imag), right_matrix(dft_real, dft_imag), left_matrix(dft_real, -dft_imag), right_matrix(dft_real, -dft_imag), chirp_real, chirp_imag)

def apply_left(matrix, field):
    batch_size = field.shape[0]
    length = field.shape[-1]
    stacked = field.reshape(batch_size, 2 * length, length)
    result = jnp.einsum('ab,nbc->nac', matrix.astype(jnp.float32), stacked.astype(jnp.float32), precision=lax.Precision.HIGHEST)
    return result.reshape(batch_size, 2, length, length)

def apply_right(matrix, field):
    length = field.shape[-1]
    result = jnp.einsum('nspq,qr->nspr', field.astype(jnp.float32), matrix.astype(jnp.float32), precision=lax.Precision.HIGHEST)
    real_out = result[:, 0, :, :length] - result[:, 1, :, length:]
    imag_out = result[:, 0, :, length:] + result[:, 1, :, :length]
    return jnp.stack([real_out, imag_out], 1)

def correct_patches(patches, measured, probe, weights, tables):
    forward_left, forward_right, back_left, back_right, chirp_real, chirp_imag = tables
    modes = probe.shape[0]
    number = patches.shape[0]
    length = probe.shape[-1]
    probe_real = probe[:, 0]
    probe_imag = probe[:, 1]
    lit_real = chirp_real * probe_real - chirp_imag * probe_imag
    lit_imag = chirp_real * probe_imag + chirp_imag * probe_real
    object_real = patches[:, 0].astype(jnp.float32)
    object_imag = patches[:, 1].astype(jnp.float32)
    exit_real = lit_real[:, None] * object_real[None] - lit_imag[:, None] * object_imag[None]
    exit_imag = lit_real[:, None] * object_imag[None] + lit_imag[:, None] * object_real[None]
    exit_wave = jnp.stack([exit_real, exit_imag], 2).astype(jnp.bfloat16).reshape(modes * number, 2, length, length)
    first_pass = apply_left(forward_left, exit_wave).astype(jnp.bfloat16)
    far_field = apply_right(forward_right, first_pass).reshape(modes, number, 2, length, length)
    intensity = lax.optimization_barrier(jnp.sum(far_field * far_field, axis=(0, 2)))
    factor = measured.astype(jnp.float32) / jnp.maximum(jnp.sqrt(intensity), AMP_FLOOR) - 1.0
    far_change = (far_field * factor[None, :, None]).astype(jnp.bfloat16).reshape(modes * number, 2, length, length)
    back_first = apply_left(back_left, far_change).astype(jnp.bfloat16)
    near_field = apply_right(back_right, back_first).reshape(modes, number, 2, length, length)
    near_real = near_field[:, :, 0]
    near_imag = near_field[:, :, 1]
    weighting = weights[None, :, None, None]
    change_real = (chirp_real * near_real + chirp_imag * near_imag) * weighting
    change_imag = (chirp_real * near_imag - chirp_imag * near_real) * weighting
    step_real = lax.optimization_barrier(jnp.sum(probe_real[:, None] * change_real + probe_imag[:, None] * change_imag, 0))
    step_imag = lax.optimization_barrier(jnp.sum(probe_real[:, None] * change_imag - probe_imag[:, None] * change_real, 0))
    patch_steps = jnp.stack([step_real, step_imag], 1).astype(jnp.bfloat16)
    grad_real = lax.optimization_barrier(jnp.sum(object_real[None] * change_real + object_imag[None] * change_imag, 1))
    grad_imag = lax.optimization_barrier(jnp.sum(object_real[None] * change_imag - object_imag[None] * change_real, 1))
    return (patch_steps, jnp.stack([grad_real, grad_imag], 1))

def reference(object_field, probe, patterns, scan_tile, scan_row, scan_col):
    length = PATCH
    tables = make_tables(length)
    row_start = (scan_tile[:, 0] * TILE_R + scan_row).astype(jnp.int32)
    blocks = SCANS // SCAN_DEV
    row_blocks = row_start.reshape(blocks, SCAN_DEV)
    col_blocks = scan_col.astype(jnp.int32).reshape(blocks, SCAN_DEV)
    pattern_blocks = patterns.reshape(blocks, SCAN_DEV, length, length)
    offsets = jnp.arange(length, dtype=jnp.int32)

    def extract(row_at, col_at):
        return lax.dynamic_slice(object_field, (jnp.int32(0), row_at, col_at), (2, length, length))

    def visit_block(totals, block_items):
        object_sum, probe_total = totals
        row_part, col_part, measured = block_items
        patches = jax.vmap(extract)(row_part, col_part).astype(jnp.bfloat16)
        weights = jnp.ones((SCAN_DEV,), jnp.float32)
        patch_steps, gradient = correct_patches(patches, measured, probe, weights, tables)
        row_index = row_part[:, None, None] + offsets[None, :, None]
        col_index = col_part[:, None, None] + offsets[None, None, :]
        object_sum = object_sum.at[:, row_index, col_index].add(jnp.moveaxis(patch_steps.astype(jnp.float32), 1, 0))
        return ((object_sum, probe_total + gradient), None)
    initial = (jnp.zeros((2, OBJ_R, OBJ_C), jnp.float32), jnp.zeros((MODES, 2, length, length), jnp.float32))
    scanned = lax.scan(visit_block, initial, (row_blocks, col_blocks, pattern_blocks))
    object_sum, probe_total = scanned[0]
    return (object_sum, probe_total * (1.0 / math.sqrt(SCANS)))
```

```python
import functools
import math

import jax
import jax.numpy as jnp
import numpy as np
from jax import lax
from jax.experimental import pallas as pl
from jax.experimental.pallas import tpu as pltpu
from jax.sharding import PartitionSpec as P

AMP_FLOOR = 0.5
HEAD = 16
DIGIT = 16
LANES = 128
BAND = 16
MAX_STAGES = 3


def dft_tables(length):
    indices = np.arange(length, dtype=np.int32)
    products = indices[:, None] * indices[None, :] % length
    angles = products.astype(np.float32) * np.float32(-2.0 * math.pi / length)
    factor = np.float32(1.0 / math.sqrt(length))
    real = (np.cos(angles) * factor).astype(jnp.bfloat16)
    imag = (np.sin(angles) * factor).astype(jnp.bfloat16)
    forward = np.block([[real, -imag], [imag, real]])
    backward = np.block([[real, imag], [-imag, real]])
    return np.stack([forward, backward])


def chirp_table(length):
    offsets = np.arange(length, dtype=np.int32) - length // 2
    squares = offsets * offsets
    phases = (squares[:, None] + squares[None, :]).astype(np.float32) * np.float32(
        0.5 * math.pi / length
    )
    return np.stack([np.cos(phases), np.sin(phases)]).astype(np.float32)


def pack_kernel(tile_count, capacity, tile_ref, row_ref, col_ref, pat_ref, *rest):
    blocks, count_ref, source_ref = rest[:tile_count], rest[tile_count], rest[tile_count + 1]
    number, length = pat_ref.shape[0], pat_ref.shape[1]
    me = lax.axis_index("tile")
    for hop in range(tile_count):
        count_ref[hop] = 0

    def place(index, carry):
        hop = tile_ref[index] ^ me
        rank = count_ref[hop]
        count_ref[hop] = rank + 1
        source_ref[hop * capacity + rank] = index
        return carry

    lax.fori_loop(0, number, place, 0)
    lane = lax.broadcasted_iota(jnp.int32, (HEAD, LANES), 1)
    line = lax.broadcasted_iota(jnp.int32, (HEAD, LANES), 0)
    for hop in range(tile_count):
        count = count_ref[hop]
        head = jnp.where(line == 4, count, 0)
        for rank in range(capacity):
            valid = rank < count
            index = jnp.where(valid, source_ref[hop * capacity + rank], 0)
            row, col = row_ref[index], col_ref[index]

            @pl.when(valid)
            def _(hop=hop, rank=rank, index=index):
                blocks[hop][rank * length : (rank + 1) * length, :] = pat_ref[index]

            digits = jnp.where(
                line == 0,
                row // DIGIT,
                jnp.where(
                    line == 1,
                    row % DIGIT,
                    jnp.where(line == 2, col // DIGIT, jnp.where(line == 3, col % DIGIT, 0)),
                ),
            )
            head = head + jnp.where((lane == rank) & valid, digits, 0)
        blocks[hop][capacity * length :, :] = head.astype(jnp.float32).astype(jnp.bfloat16)


def pack(patterns, tile_ids, rows, cols, tile_count, capacity):
    length = patterns.shape[-1]
    block = jax.ShapeDtypeStruct((capacity * length + HEAD, length), jnp.bfloat16)
    smem = pl.BlockSpec(memory_space=pltpu.SMEM)
    vmem = pl.BlockSpec(memory_space=pltpu.VMEM)
    return pl.pallas_call(
        functools.partial(pack_kernel, tile_count, capacity),
        out_shape=[block] * tile_count,
        in_specs=[smem, smem, smem, vmem],
        out_specs=[vmem] * tile_count,
        scratch_shapes=[
            pltpu.SMEM((tile_count,), jnp.int32),
            pltpu.SMEM((tile_count * capacity,), jnp.int32),
        ],
        compiler_params=pltpu.CompilerParams(vmem_limit_bytes=24 * 2**20),
        name="pack_patterns",
    )(tile_ids, rows, cols, patterns)


def step_kernel(block_count, capacity, scale, width, object_hbm, probe_ref, dft_ref, chirp_ref, *rest):
    blocks = rest[:block_count]
    keep_hbm, send_hbm, grad_keep_hbm, grad_send_hbm = rest[block_count : block_count + 4]
    (
        field,
        total,
        pats,
        heads,
        corners,
        list_row,
        list_col,
        list_pat,
        lit,
        grad,
        patch,
        wide,
        tall,
        far,
        in_sem,
        out_sem,
    ) = rest[block_count + 4 :]
    modes, _, length, _ = probe_ref.shape
    rows, columns = object_hbm.shape[1:]
    block_rows = capacity * length + HEAD
    bands = length // BAND
    pos = lax.axis_index("pos")

    column_tiles = columns // LANES
    load_field = [
        pltpu.make_async_copy(
            object_hbm.at[:, :, tile * LANES : (tile + 1) * LANES],
            field.at[:, tile, 0:rows, :],
            in_sem.at[block_count + 1 + tile],
        )
        for tile in range(column_tiles)
    ]
    loads = [
        pltpu.make_async_copy(
            blocks[b], pats.at[b * block_rows : (b + 1) * block_rows], in_sem.at[b]
        )
        for b in range(block_count)
    ]
    for load in loads + load_field:
        load.start()

    def clear(index, carry):
        at = pl.ds(pl.multiple_of(index * 8, 8), 8)
        for plane in range(2):
            for tile in range(column_tiles + 1):
                total[plane, tile, at, :] = jnp.zeros((8, LANES), jnp.float32)
        return carry

    lax.fori_loop(0, total.shape[2] // 8, clear, 0)
    for mode in range(modes):
        for band in range(bands):
            at = pl.ds(band * BAND, BAND)
            cr, ci = chirp_ref[0, at, :], chirp_ref[1, at, :]
            pr, pi = probe_ref[mode, 0, at, :], probe_ref[mode, 1, at, :]
            lit[mode, 0, at, :] = cr * pr - ci * pi
            lit[mode, 1, at, :] = cr * pi + ci * pr
            grad[pl.ds((2 * mode) * length + band * BAND, BAND), :] = jnp.zeros_like(cr)
            grad[pl.ds((2 * mode + 1) * length + band * BAND, BAND), :] = jnp.zeros_like(cr)

    for load in loads:
        load.wait()
    for b in range(block_count):
        heads[b * HEAD : (b + 1) * HEAD, :] = (
            pats[(b + 1) * block_rows - HEAD : (b + 1) * block_rows, :]
            .astype(jnp.float32)
            .astype(jnp.int32)
        )
    fetch = pltpu.make_async_copy(heads, corners, in_sem.at[block_count])
    fetch.start()
    fetch.wait()

    number = jnp.int32(0)
    for b in range(block_count):

        def note(rank, at, b=b):
            first = b * HEAD
            list_row[at] = corners[first, rank] * DIGIT + corners[first + 1, rank]
            list_col[at] = corners[first + 2, rank] * DIGIT + corners[first + 3, rank]
            list_pat[at] = b * block_rows + rank * length
            return at + 1

        number = lax.fori_loop(0, corners[b * HEAD + 4, 0], note, number)
    for load in load_field:
        load.wait()

    lane = lax.broadcasted_iota(jnp.int32, (BAND, LANES), 1)

    def visit(turn, carry):
        items = []
        for u in range(width):
            index = turn * width + u
            valid = index < number
            index = jnp.where(valid, index, turn * width)
            col = list_col[index]
            shift = col % LANES
            items.append(
                (
                    u,
                    list_row[index],
                    col // LANES,
                    shift,
                    pl.multiple_of(list_pat[index], LANES),
                    jnp.where(valid, jnp.float32(1.0), jnp.float32(0.0)),
                )
            )
        for u, row, col, shift, _, _ in items:
            back = (LANES - shift) % LANES
            inside = lane < LANES - shift
            for band in range(bands):
                at = pl.ds(band * BAND, BAND)
                at_field = pl.ds(row + band * BAND, BAND)
                planes = []
                for plane in range(2):
                    left = pltpu.roll(field[plane, col, at_field, :], back, 1)
                    right = pltpu.roll(field[plane, col + 1, at_field, :], back, 1)
                    cell = jnp.where(inside, left, right).astype(jnp.bfloat16).astype(jnp.float32)
                    patch[u, plane, at, :] = cell
                    planes.append(cell)
                pr, pi = planes
                for mode in range(modes):
                    lr, li = lit[mode, 0, at, :], lit[mode, 1, at, :]
                    lanes = pl.ds(mode * length, length)
                    wide[u, pl.ds(band * BAND, BAND), lanes] = (lr * pr - li * pi).astype(
                        jnp.bfloat16
                    )
                    wide[u, pl.ds(length + band * BAND, BAND), lanes] = (
                        lr * pi + li * pr
                    ).astype(jnp.bfloat16)

        def columns_pass(u, table):
            for mode in range(0, modes, 2):
                both = min(2, modes - mode)
                out = jnp.dot(
                    dft_ref[table],
                    wide[u, :, mode * length : (mode + both) * length],
                    preferred_element_type=jnp.float32,
                ).astype(jnp.bfloat16)
                for q in range(both):
                    at = pl.ds((mode + q) * length, length)
                    tall[u, at, 0:length] = out[0:length, q * length : (q + 1) * length]
                    tall[u, at, length : 2 * length] = out[
                        length : 2 * length, q * length : (q + 1) * length
                    ]

        def rows_pass(u, table):
            far[u] = jnp.dot(tall[u], dft_ref[table], preferred_element_type=jnp.float32)

        for item in items:
            columns_pass(item[0], 0)
        for item in items:
            rows_pass(item[0], 1)
        for u, _, _, _, source, weight in items:
            for band in range(bands):
                waves = []
                bright = None
                for mode in range(modes):
                    at = pl.ds(mode * length + band * BAND, BAND)
                    fr, fi = far[u, at, 0:length], far[u, at, length : 2 * length]
                    waves.append((fr, fi))
                    power = fr * fr + fi * fi
                    bright = power if bright is None else bright + power
                measured = pats[pl.ds(source + band * BAND, BAND), :].astype(jnp.float32)
                inverse = jnp.minimum(lax.rsqrt(bright), 1.0 / AMP_FLOOR)
                factor = (measured * inverse - 1.0) * weight
                for mode in range(modes):
                    fr, fi = waves[mode]
                    lanes = pl.ds(mode * length, length)
                    wide[u, pl.ds(band * BAND, BAND), lanes] = (fr * factor).astype(jnp.bfloat16)
                    wide[u, pl.ds(length + band * BAND, BAND), lanes] = (fi * factor).astype(
                        jnp.bfloat16
                    )
        for item in items:
            columns_pass(item[0], 1)
        for item in items:
            rows_pass(item[0], 0)
        for band in range(bands):
            at = pl.ds(band * BAND, BAND)
            steps = [[None, None] for _ in items]
            for mode in range(modes):
                at_far = pl.ds(mode * length + band * BAND, BAND)
                at_gr = pl.ds((2 * mode) * length + band * BAND, BAND)
                at_gi = pl.ds((2 * mode + 1) * length + band * BAND, BAND)
                lr, li = lit[mode, 0, at, :], lit[mode, 1, at, :]
                gr, gi = grad[at_gr, :], grad[at_gi, :]
                for item in items:
                    u = item[0]
                    nr, ni = far[u, at_far, 0:length], far[u, at_far, length : 2 * length]
                    pr, pi = patch[u, 0, at, :], patch[u, 1, at, :]
                    sr, si = lr * nr + li * ni, lr * ni - li * nr
                    if mode:
                        sr, si = steps[u][0] + sr, steps[u][1] + si
                    steps[u] = [sr, si]
                    gr = gr + (pr * nr + pi * ni)
                    gi = gi + (pr * ni - pi * nr)
                grad[at_gr, :] = gr
                grad[at_gi, :] = gi
            for u, row, col, shift, _, _ in items:
                at_field = pl.ds(row + band * BAND, BAND)
                for plane in range(2):
                    step = steps[u][plane].astype(jnp.bfloat16).astype(jnp.float32)
                    moved = pltpu.roll(step, shift, 1)
                    total[plane, col, at_field, :] += jnp.where(lane >= shift, moved, 0.0)
                    total[plane, col + 1, at_field, :] += jnp.where(lane < shift, moved, 0.0)
        return carry

    lax.fori_loop(0, (number + width - 1) // width, visit, 0)

    for mode in range(modes):
        for band in range(bands):
            at = pl.ds(band * BAND, BAND)
            at_gr = pl.ds((2 * mode) * length + band * BAND, BAND)
            at_gi = pl.ds((2 * mode + 1) * length + band * BAND, BAND)
            cr, ci = chirp_ref[0, at, :] * scale, chirp_ref[1, at, :] * scale
            gr, gi = grad[at_gr, :], grad[at_gi, :]
            grad[at_gr, :] = cr * gr + ci * gi
            grad[at_gi, :] = cr * gi - ci * gr
    half = column_tiles // 2
    grad_half = grad.shape[0] // 2
    stores = []
    for grad_out, out, side in (
        (grad_send_hbm, send_hbm, 1 - pos),
        (grad_keep_hbm, keep_hbm, pos),
    ):
        stores.append(
            pltpu.make_async_copy(
                grad.at[pl.ds(pl.multiple_of(side * grad_half, 8), grad_half), :],
                grad_out,
                out_sem.at[len(stores)],
            )
        )
        for tile in range(half):
            stores.append(
                pltpu.make_async_copy(
                    total.at[:, side * half + tile, 0:rows, :],
                    out.at[:, :, tile * LANES : (tile + 1) * LANES],
                    out_sem.at[len(stores)],
                )
            )
    for store in stores:
        store.start()
    for store in stores:
        store.wait()


def step(object_field, probe, blocks, tables, scale, capacity):
    modes, _, length, _ = probe.shape
    rows, columns = object_field.shape[1:]
    count = len(blocks)
    width = 2
    slots = count * capacity
    vmem = pl.BlockSpec(memory_space=pltpu.VMEM)
    hbm = pl.BlockSpec(memory_space=pl.ANY)
    f32, bf16 = jnp.float32, jnp.bfloat16
    padded = (2, columns // LANES + 1, rows + 8, LANES)
    work = slots * modes * 4 * 8 * length**3
    return pl.pallas_call(
        functools.partial(step_kernel, count, capacity, scale, width),
        out_shape=[
            jax.ShapeDtypeStruct((2, rows, columns // 2), f32),
            jax.ShapeDtypeStruct((2, rows, columns // 2), f32),
            jax.ShapeDtypeStruct((modes * length, length), f32),
            jax.ShapeDtypeStruct((modes * length, length), f32),
        ],
        in_specs=[hbm, vmem, vmem, vmem] + [hbm] * count,
        out_specs=[hbm] * 4,
        scratch_shapes=[
            pltpu.VMEM(padded, f32),
            pltpu.VMEM(padded, f32),
            pltpu.VMEM((count * (capacity * length + HEAD), length), bf16),
            pltpu.VMEM((count * HEAD, LANES), jnp.int32),
            pltpu.SMEM((count * HEAD, LANES), jnp.int32),
            pltpu.SMEM((slots,), jnp.int32),
            pltpu.SMEM((slots,), jnp.int32),
            pltpu.SMEM((slots,), jnp.int32),
            pltpu.VMEM((modes, 2, length, length), f32),
            pltpu.VMEM((2 * modes * length, length), f32),
            pltpu.VMEM((width, 2, length, length), f32),
            pltpu.VMEM((width, 2 * length, modes * length), bf16),
            pltpu.VMEM((width, modes * length, 2 * length), bf16),
            pltpu.VMEM((width, modes * length, 2 * length), f32),
            pltpu.SemaphoreType.DMA((count + 1 + columns // LANES,)),
            pltpu.SemaphoreType.DMA((2 + columns // LANES,)),
        ],
        compiler_params=pltpu.CompilerParams(vmem_limit_bytes=40 * 2**20),
        cost_estimate=pl.CostEstimate(
            flops=work, bytes_accessed=16 * 2**20, transcendentals=slots * length**2
        ),
        name="gradient_step",
    )(object_field, probe, *tables, *blocks)


def sum_over_scans(keep, send, tile_count):
    other = [(0, 1), (1, 0)]
    part = keep + lax.ppermute(send, "pos", other)
    rows, length = part.shape
    pieces = part.reshape(tile_count, rows // tile_count, length)
    mine = jnp.sum(lax.all_to_all(pieces, "tile", split_axis=0, concat_axis=0, tiled=True), 0)
    copies = jnp.broadcast_to(mine[None], pieces.shape)
    whole = lax.all_to_all(copies, "tile", split_axis=0, concat_axis=0, tiled=True)
    whole = whole.reshape(rows, length)
    return (whole, lax.ppermute(whole, "pos", other))


def on_device(object_field, probe, patterns, scan_tile, scan_row, scan_col):
    tile_count = lax.axis_size("tile")
    pos_count = lax.axis_size("pos")
    number, length = patterns.shape[0], patterns.shape[-1]
    capacity = max(2, 2 * number // tile_count)
    scale = 1.0 / math.sqrt(number * tile_count * pos_count)
    tables = (jnp.asarray(dft_tables(length)), jnp.asarray(chirp_table(length)))
    blocks = pack(patterns, scan_tile[:, 0], scan_row, scan_col, tile_count, capacity)
    arrived = [blocks[0]]
    for hop in range(1, tile_count):
        arrived.append(
            lax.ppermute(blocks[hop], "tile", [(i, i ^ hop) for i in range(tile_count)])
        )
    cuts = [0, tile_count // 2, tile_count * 3 // 4, tile_count]
    parts = [
        step(object_field, probe, arrived[a:b], tables, scale, capacity)
        for a, b in zip(cuts[:-1], cuts[1:])
    ]
    keep, send, grad_keep, grad_send = [sum(group[1:], group[0]) for group in zip(*parts)]
    mine, theirs = sum_over_scans(grad_keep, grad_send, tile_count)
    first = lax.axis_index("pos") == 0
    grad = jnp.concatenate([jnp.where(first, mine, theirs), jnp.where(first, theirs, mine)])
    object_step = keep + lax.ppermute(send, "pos", [(0, 1), (1, 0)])
    return (object_step, grad.reshape(probe.shape))


def solution(mesh):
    placed = (
        P("groups", "tile", None),
        P("groups", None, None, None),
        P(("groups", "tile", "pos"), None, None),
        P(("groups", "tile", "pos"), None),
        P(("groups", "tile", "pos")),
        P(("groups", "tile", "pos")),
    )
    return jax.shard_map(
        on_device,
        mesh=mesh,
        in_specs=placed,
        out_specs=(P("groups", "tile", "pos"), P("groups", None, None, None)),
        check_vma=False,
    )
```

```python
import functools
import math

import jax
import jax.numpy as jnp
import numpy as np
from jax import lax
from jax.experimental import pallas as pl
from jax.experimental.pallas import tpu as pltpu
from jax.sharding import PartitionSpec as P

AMP_FLOOR = 0.5
HEAD = 16
DIGIT = 16
LANES = 128
SQUARE = 4
CROSS = jnp.float32
BAND = 16


def dft_tables(length):
    indices = np.arange(length, dtype=np.int32)
    products = indices[:, None] * indices[None, :] % length
    angles = products.astype(np.float32) * np.float32(-2.0 * math.pi / length)
    factor = np.float32(1.0 / math.sqrt(length))
    real = (np.cos(angles) * factor).astype(jnp.bfloat16)
    imag = (np.sin(angles) * factor).astype(jnp.bfloat16)
    forward = np.block([[real, -imag], [imag, real]])
    backward = np.block([[real, imag], [-imag, real]])
    return np.stack([forward, backward])


def chirp_table(length):
    offsets = np.arange(length, dtype=np.int32) - length // 2
    squares = offsets * offsets
    phases = (squares[:, None] + squares[None, :]).astype(np.float32) * np.float32(
        0.5 * math.pi / length
    )
    return np.stack([np.cos(phases), np.sin(phases)]).astype(np.float32)


def pack_kernel(tile_count, capacity, tile_ref, row_ref, col_ref, pat_ref, *rest):
    blocks, count_ref, source_ref = rest[:tile_count], rest[tile_count], rest[tile_count + 1]
    number, length = pat_ref.shape[0], pat_ref.shape[1]
    me = lax.axis_index("tile")
    for hop in range(tile_count):
        count_ref[hop] = 0

    def place(index, carry):
        hop = tile_ref[index] ^ me
        rank = count_ref[hop]
        count_ref[hop] = rank + 1
        source_ref[hop * capacity + rank] = index
        return carry

    lax.fori_loop(0, number, place, 0)
    lane = lax.broadcasted_iota(jnp.int32, (HEAD, LANES), 1)
    line = lax.broadcasted_iota(jnp.int32, (HEAD, LANES), 0)
    for hop in range(tile_count):
        count = count_ref[hop]
        head = jnp.where(line == 4, count, 0)
        for rank in range(capacity):
            valid = rank < count
            index = jnp.where(valid, source_ref[hop * capacity + rank], 0)
            row, col = row_ref[index], col_ref[index]

            @pl.when(valid)
            def _(hop=hop, rank=rank, index=index):
                blocks[hop][rank * length : (rank + 1) * length, :] = pat_ref[index]

            digits = jnp.where(
                line == 0,
                row // DIGIT,
                jnp.where(
                    line == 1,
                    row % DIGIT,
                    jnp.where(line == 2, col // DIGIT, jnp.where(line == 3, col % DIGIT, 0)),
                ),
            )
            head = head + jnp.where((lane == rank) & valid, digits, 0)
        blocks[hop][capacity * length :, :] = head.astype(jnp.float32).astype(jnp.bfloat16)


def pack(patterns, tile_ids, rows, cols, tile_count, capacity):
    length = patterns.shape[-1]
    block = jax.ShapeDtypeStruct((capacity * length + HEAD, length), jnp.bfloat16)
    smem = pl.BlockSpec(memory_space=pltpu.SMEM)
    vmem = pl.BlockSpec(memory_space=pltpu.VMEM)
    return pl.pallas_call(
        functools.partial(pack_kernel, tile_count, capacity),
        out_shape=[block] * tile_count,
        in_specs=[smem, smem, smem, vmem],
        out_specs=[vmem] * tile_count,
        scratch_shapes=[
            pltpu.SMEM((tile_count,), jnp.int32),
            pltpu.SMEM((tile_count * capacity,), jnp.int32),
        ],
        compiler_params=pltpu.CompilerParams(vmem_limit_bytes=56 * 2**20),
        name="pack_patterns",
    )(tile_ids, rows, cols, patterns)


def step_kernel(
    block_count, capacity, scale, first, last, object_hbm, probe_ref, dft_ref, chirp_ref, *rest
):
    blocks = rest[:block_count]
    rest = rest[block_count:]
    if not first:
        before = rest[:SQUARE]
        rest = rest[SQUARE:]
    after = rest[: 2 + SQUARE]
    (
        field,
        total,
        pats,
        heads,
        corners,
        list_row,
        list_col,
        list_pat,
        lit,
        grad,
        patch_even,
        patch_odd,
        wide,
        tall,
        in_sem,
        out_sem,
    ) = rest[2 + SQUARE :]
    modes, _, length, _ = probe_ref.shape
    rows, columns = object_hbm.shape[1:]
    block_rows = capacity * length + HEAD
    bands = length // BAND
    pos = lax.axis_index("pos")

    column_tiles = columns // LANES
    load_field = [
        pltpu.make_async_copy(
            object_hbm.at[:, :, tile * LANES : (tile + 1) * LANES],
            field.at[:, tile, 0:rows, :],
            in_sem.at[block_count + 1 + tile],
        )
        for tile in range(column_tiles)
    ]
    loads = [
        pltpu.make_async_copy(
            blocks[b], pats.at[b * block_rows : (b + 1) * block_rows], in_sem.at[b]
        )
        for b in range(block_count)
    ]
    for load in loads + load_field:
        load.start()

    half = column_tiles // 2
    quarter = grad.shape[0] // SQUARE
    me = lax.axis_index("tile") % (SQUARE // 2) * 2 + pos

    def grad_parts(outsides):
        return [
            (grad.at[pl.ds(pl.multiple_of((me ^ turn) * quarter, 8), quarter), :], outside)
            for turn, outside in enumerate(outsides)
        ]

    def total_parts(keep_out, send_out):
        return [
            (
                total.at[:, side * half + tile, 0:rows, :],
                out.at[:, :, tile * LANES : (tile + 1) * LANES],
            )
            for out, side in ((send_out, 1 - pos), (keep_out, pos))
            for tile in range(half)
        ]

    carried = []
    if first:
        grad[...] = jnp.zeros_like(grad)
    else:
        carried = [
            pltpu.make_async_copy(outside, inside, out_sem.at[n])
            for n, (inside, outside) in enumerate(grad_parts(before))
        ]
    for load in carried:
        load.start()

    def clear(index, carry):
        at = pl.ds(pl.multiple_of(index * 8, 8), 8)
        for plane in range(2):
            for tile in range(column_tiles):
                total[plane, tile, at, :] = jnp.zeros((8, LANES), jnp.float32)
        return carry

    lax.fori_loop(0, rows // 8, clear, 0)
    for mode in range(modes):
        for band in range(bands):
            at = pl.ds(band * BAND, BAND)
            cr, ci = chirp_ref[0, at, :], chirp_ref[1, at, :]
            pr, pi = probe_ref[mode, 0, at, :], probe_ref[mode, 1, at, :]
            lit[mode, 0, at, :] = cr * pr - ci * pi
            lit[mode, 1, at, :] = cr * pi + ci * pr

    for load in loads:
        load.wait()
    for b in range(block_count):
        heads[b * HEAD : (b + 1) * HEAD, :] = (
            pats[(b + 1) * block_rows - HEAD : (b + 1) * block_rows, :]
            .astype(jnp.float32)
            .astype(jnp.int32)
        )
    fetch = pltpu.make_async_copy(heads, corners, in_sem.at[block_count])
    fetch.start()
    fetch.wait()

    number = jnp.int32(0)
    for b in range(block_count):

        def note(rank, at, b=b):
            first = b * HEAD
            list_row[at] = corners[first, rank] * DIGIT + corners[first + 1, rank]
            list_col[at] = corners[first + 2, rank] * DIGIT + corners[first + 3, rank]
            list_pat[at] = b * block_rows + rank * length
            return at + 1

        number = lax.fori_loop(0, corners[b * HEAD + 4, 0], note, number)
    for load in load_field + carried:
        load.wait()

    patch = (patch_even, patch_odd)
    group = max(BAND, LANES // modes)
    groups = length // group
    tall_rows = modes * group

    def item(index):
        index = jnp.clip(index, 0, number - 1)
        row, col = list_row[index], list_col[index]
        shift = col % LANES
        return row, col // LANES, shift, pl.multiple_of(list_pat[index], LANES)

    def exit_chunks(index, side):
        row, col, shift, _ = item(index)
        slot = (index >> 1) & 1
        back = (LANES - shift) % LANES

        def chunk(band):
            at = pl.ds(band * BAND, BAND)
            at_field = pl.ds(row + band * BAND, BAND)
            lane = lax.broadcasted_iota(jnp.int32, (BAND, LANES), 1)
            planes = []
            for plane in range(2):
                left = pltpu.roll(field[plane, col, at_field, :], back, 1)
                right = pltpu.roll(field[plane, col + 1, at_field, :], back, 1)
                cell = jnp.where(lane < LANES - shift, left, right)
                cell = cell.astype(jnp.bfloat16).astype(jnp.float32)
                patch[side][slot, plane, at, :] = cell
                planes.append(cell)
            pr, pi = planes
            for mode in range(modes):
                lr, li = lit[mode, 0, at, :], lit[mode, 1, at, :]
                lanes = pl.ds(mode * length, length)
                wide[side, at, lanes] = (lr * pr - li * pi).astype(jnp.bfloat16)
                wide[side, pl.ds(length + band * BAND, BAND), lanes] = (
                    lr * pi + li * pr
                ).astype(jnp.bfloat16)

        return [functools.partial(chunk, band) for band in range(bands)]

    def column_chunks(source, target, table):
        def chunk(mode):
            both = min(2, modes - mode)
            out = jnp.dot(
                dft_ref[table],
                wide[source, :, mode * length : (mode + both) * length],
                preferred_element_type=jnp.float32,
            ).astype(jnp.bfloat16)
            for q in range(both):
                for g in range(groups):
                    at = pl.ds(g * tall_rows + (mode + q) * group, group)
                    for plane in range(2):
                        tall[target, at, plane * length : (plane + 1) * length] = out[
                            plane * length + g * group : plane * length + (g + 1) * group,
                            q * length : (q + 1) * length,
                        ]

        return [functools.partial(chunk, mode) for mode in range(0, modes, 2)]

    def row_product(source, table, g):
        out = jnp.dot(
            tall[source, g * tall_rows : (g + 1) * tall_rows, :],
            dft_ref[table],
            preferred_element_type=jnp.float32,
        )
        return [
            (
                out[mode * group : (mode + 1) * group, 0:length],
                out[mode * group : (mode + 1) * group, length : 2 * length],
            )
            for mode in range(modes)
        ]

    def far_chunks(index, side):
        _, _, _, source = item(index)
        weight = jnp.where((index >= 0) & (index < number), jnp.float32(1.0), jnp.float32(0.0))

        def chunk(g):
            waves = row_product(side, 1, g)
            bright = None
            for fr, fi in waves:
                power = fr * fr + fi * fi
                bright = power if bright is None else bright + power
            measured = pats[pl.ds(source + g * group, group), :].astype(jnp.float32)
            inverse = jnp.minimum(lax.rsqrt(bright), 1.0 / AMP_FLOOR)
            factor = (measured * inverse - 1.0) * weight
            for mode in range(modes):
                fr, fi = waves[mode]
                lanes = pl.ds(mode * length, length)
                wide[2, pl.ds(g * group, group), lanes] = (fr * factor).astype(jnp.bfloat16)
                wide[2, pl.ds(length + g * group, group), lanes] = (fi * factor).astype(
                    jnp.bfloat16
                )

        return [functools.partial(chunk, g) for g in range(groups)]

    def step_chunks(index, side):
        row, col, shift, _ = item(index)
        slot = (index >> 1) & 1

        def chunk(g):
            at = pl.ds(g * group, group)
            at_field = pl.ds(row + g * group, group)
            lane = lax.broadcasted_iota(jnp.int32, (group, LANES), 1)
            waves = row_product(2 + side, 0, g)
            pr, pi = patch[side][slot, 0, at, :], patch[side][slot, 1, at, :]
            steps = [None, None]
            for mode in range(modes):
                at_gr = pl.ds((2 * mode) * length + g * group, group)
                at_gi = pl.ds((2 * mode + 1) * length + g * group, group)
                lr, li = lit[mode, 0, at, :], lit[mode, 1, at, :]
                nr, ni = waves[mode]
                sr, si = lr * nr + li * ni, lr * ni - li * nr
                steps = [sr, si] if mode == 0 else [steps[0] + sr, steps[1] + si]
                grad[at_gr, :] += pr * nr + pi * ni
                grad[at_gi, :] += pr * ni - pi * nr
            places = [(plane, col + tile) for plane in range(2) for tile in range(2)]
            olds = [total[plane, tile, at_field, :] for plane, tile in places]
            sums = []
            for plane in range(2):
                moved = steps[plane].astype(jnp.bfloat16).astype(jnp.float32)
                moved = pltpu.roll(moved, shift, 1)
                sums.append(olds[2 * plane] + jnp.where(lane >= shift, moved, 0.0))
                sums.append(olds[2 * plane + 1] + jnp.where(lane < shift, moved, 0.0))
            for (plane, tile), value in zip(places, sums):
                total[plane, tile, at_field, :] = value

        return [functools.partial(chunk, g) for g in range(groups)]

    def run(*lists):
        order = []
        for rank, chunks in enumerate(lists):
            order += [((n + 0.5) / len(chunks), rank, chunk) for n, chunk in enumerate(chunks)]
        for _, _, chunk in sorted(order, key=lambda entry: entry[:2]):
            chunk()

    def visit(turn, carry):
        for side in range(2):
            at, other = 2 * turn + side, 1 - side
            run(far_chunks(at, side))
            run(column_chunks(other, other, 0), exit_chunks(at + 2, side))
            run(column_chunks(2, 2 + side, 1), step_chunks(at - 1, other))
        return carry

    @pl.when(number > 0)
    def _():
        tall[3] = jnp.zeros(tall.shape[1:], tall.dtype)
        patch[1][1] = jnp.zeros(patch[1].shape[1:], jnp.float32)
        run(exit_chunks(jnp.int32(0), 0))
        run(column_chunks(0, 0, 0), exit_chunks(jnp.int32(1), 1))
        lax.fori_loop(0, number // 2 + 1, visit, 0)

    for mode in range(modes if last else 0):
        for band in range(bands):
            at = pl.ds(band * BAND, BAND)
            at_gr = pl.ds((2 * mode) * length + band * BAND, BAND)
            at_gi = pl.ds((2 * mode + 1) * length + band * BAND, BAND)
            cr, ci = chirp_ref[0, at, :] * scale, chirp_ref[1, at, :] * scale
            gr, gi = grad[at_gr, :], grad[at_gi, :]
            grad[at_gr, :] = cr * gr + ci * gi
            grad[at_gi, :] = cr * gi - ci * gr
    stores = [
        pltpu.make_async_copy(inside, outside, out_sem.at[n])
        for n, (inside, outside) in enumerate(
            grad_parts(after[2:]) + total_parts(*after[:2])
        )
    ]
    for store in stores:
        store.start()
    for store in stores:
        store.wait()


def step(object_field, probe, blocks, tables, scale, capacity, before=None, last=True):
    modes, _, length, _ = probe.shape
    rows, columns = object_field.shape[1:]
    count = len(blocks)
    slots = count * capacity
    vmem = pl.BlockSpec(memory_space=pltpu.VMEM)
    hbm = pl.BlockSpec(memory_space=pl.ANY)
    f32, bf16 = jnp.float32, jnp.bfloat16
    padded = (2, columns // LANES + 1, rows + 8, LANES)
    work = slots * modes * 4 * 8 * length**3
    return pl.pallas_call(
        functools.partial(
            step_kernel, count, capacity, scale, before is None, last
        ),
        out_shape=[
            jax.ShapeDtypeStruct((2, rows, columns // 2), f32),
            jax.ShapeDtypeStruct((2, rows, columns // 2), f32),
        ]
        + [jax.ShapeDtypeStruct((2 * modes * length // SQUARE, length), f32)] * SQUARE,
        in_specs=[hbm, vmem, vmem, vmem] + [hbm] * (count + len(before or ())),
        out_specs=[hbm] * (2 + SQUARE),
        scratch_shapes=[
            pltpu.VMEM(padded, f32),
            pltpu.VMEM(padded, f32),
            pltpu.VMEM((count * (capacity * length + HEAD), length), bf16),
            pltpu.VMEM((count * HEAD, LANES), jnp.int32),
            pltpu.SMEM((count * HEAD, LANES), jnp.int32),
            pltpu.SMEM((slots,), jnp.int32),
            pltpu.SMEM((slots,), jnp.int32),
            pltpu.SMEM((slots,), jnp.int32),
            pltpu.VMEM((modes, 2, length, length), f32),
            pltpu.VMEM((2 * modes * length, length), f32),
            pltpu.VMEM((2, 2, length, length), f32),
            pltpu.VMEM((2, 2, length, length), f32),
            pltpu.VMEM((3, 2 * length, modes * length), bf16),
            pltpu.VMEM((4, modes * length, 2 * length), bf16),
            pltpu.SemaphoreType.DMA((count + 1 + columns // LANES,)),
            pltpu.SemaphoreType.DMA((SQUARE + columns // LANES,)),
        ],
        compiler_params=pltpu.CompilerParams(vmem_limit_bytes=56 * 2**20),
        cost_estimate=pl.CostEstimate(
            flops=work, bytes_accessed=16 * 2**20, transcendentals=slots * length**2
        ),
        name="gradient_step",
    )(object_field, probe, *tables, *blocks, *(before or ()))


def from_peer(array, turn, devices):
    pairs = [(i, i ^ turn) for i in range(devices)]
    return lax.ppermute(array, ("tile", "pos"), pairs)


def tree_sum(parts):
    while len(parts) > 1:
        parts = [a + b for a, b in zip(parts[::2], parts[1::2])]
    return parts[0]


def on_device(object_field, probe, patterns, scan_tile, scan_row, scan_col):
    tile_count = lax.axis_size("tile")
    pos_count = lax.axis_size("pos")
    number, length = patterns.shape[0], patterns.shape[-1]
    capacity = max(2, 2 * number // tile_count)
    scale = 1.0 / math.sqrt(number * tile_count * pos_count)
    tables = (jnp.asarray(dft_tables(length)), jnp.asarray(chirp_table(length)))
    blocks = pack(patterns, scan_tile[:, 0], scan_row, scan_col, tile_count, capacity)
    late = tile_count * 3 // 4
    order = [*range(late - tile_count // 4), *range(late, tile_count), *range(tile_count // 2, late)]
    arrived = [blocks[0]]
    for hop in order[1:]:
        block = blocks[hop]
        if len(arrived) >= late:
            block = lax.optimization_barrier((block, arrived[1]))[0]
        arrived.append(lax.ppermute(block, "tile", [(i, i ^ hop) for i in range(tile_count)]))
    cuts = [0, tile_count // 2, tile_count * 3 // 4, tile_count]
    grads, keeps, sends = None, [], []
    for a, b in zip(cuts[:-1], cuts[1:]):
        keep, send, *grads = step(
            object_field, probe, arrived[a:b], tables, scale, capacity, grads, b == tile_count
        )
        keeps.append(keep)
        sends.append(send)

    devices = tile_count * pos_count
    inside, across = range(1, SQUARE), range(SQUARE, devices, SQUARE)
    part = tree_sum([grads[0]] + [from_peer(grads[turn], turn, devices) for turn in inside])
    sends[-1], part = lax.optimization_barrier((sends[-1], part))
    other = [(0, 1), (1, 0)]
    object_step = sum(keeps[1:], keeps[0])
    for send in sends:
        object_step = object_step + lax.ppermute(send, "pos", other)
    part = part.astype(CROSS)
    part = tree_sum(
        [part.astype(jnp.float32)]
        + [from_peer(part, turn, devices).astype(jnp.float32) for turn in across]
    )
    part, object_step = lax.optimization_barrier((part, object_step))
    square = [part] + [from_peer(part, turn, devices) for turn in inside]
    me = lax.axis_index(("tile", "pos"))
    for bit in (1, 2):
        swapped = (me & bit) != 0
        square = [jnp.where(swapped, square[q ^ bit], square[q]) for q in range(SQUARE)]
    return (object_step, jnp.concatenate(square).reshape(probe.shape))


def solution(mesh):
    placed = (
        P("groups", "tile", None),
        P("groups", None, None, None),
        P(("groups", "tile", "pos"), None, None),
        P(("groups", "tile", "pos"), None),
        P(("groups", "tile", "pos")),
        P(("groups", "tile", "pos")),
    )
    return jax.shard_map(
        on_device,
        mesh=mesh,
        in_specs=placed,
        out_specs=(P("groups", "tile", "pos"), P("groups", None, None, None)),
        check_vma=False,
    )
```

```python
import functools
import math

import jax
import jax.numpy as jnp
import numpy as np
from jax import lax
from jax.experimental import pallas as pl
from jax.experimental.pallas import tpu as pltpu
from jax.sharding import PartitionSpec as P

AMP_FLOOR = 0.5
HEAD = 16
DIGIT = 16
LANES = 128
SQUARE = 4

BAND = 16


def dft_tables(length):
    indices = np.arange(length, dtype=np.int32)
    products = indices[:, None] * indices[None, :] % length
    angles = products.astype(np.float32) * np.float32(-2.0 * math.pi / length)
    factor = np.float32(1.0 / math.sqrt(length))
    real = (np.cos(angles) * factor).astype(jnp.bfloat16)
    imag = (np.sin(angles) * factor).astype(jnp.bfloat16)
    forward = np.block([[real, -imag], [imag, real]])
    backward = np.block([[real, imag], [-imag, real]])
    return np.stack([forward, backward])


def chirp_table(length):
    offsets = np.arange(length, dtype=np.int32) - length // 2
    squares = offsets * offsets
    phases = (squares[:, None] + squares[None, :]).astype(np.float32) * np.float32(
        0.5 * math.pi / length
    )
    return np.stack([np.cos(phases), np.sin(phases)]).astype(np.float32)


def pack_kernel(tile_count, capacity, tile_ref, row_ref, col_ref, pat_ref, *rest):
    blocks, count_ref, source_ref = rest[:tile_count], rest[tile_count], rest[tile_count + 1]
    number, length = pat_ref.shape[0], pat_ref.shape[1]
    me = lax.axis_index("tile")
    for hop in range(tile_count):
        count_ref[hop] = 0

    def place(index, carry):
        hop = tile_ref[index] ^ me
        rank = count_ref[hop]
        count_ref[hop] = rank + 1
        source_ref[hop * capacity + rank] = index
        return carry

    lax.fori_loop(0, number, place, 0)
    lane = lax.broadcasted_iota(jnp.int32, (HEAD, LANES), 1)
    line = lax.broadcasted_iota(jnp.int32, (HEAD, LANES), 0)
    for hop in range(tile_count):
        count = count_ref[hop]
        head = jnp.where(line == 4, count, 0)
        for rank in range(capacity):
            valid = rank < count
            index = jnp.where(valid, source_ref[hop * capacity + rank], 0)
            row, col = row_ref[index], col_ref[index]

            @pl.when(valid)
            def _(hop=hop, rank=rank, index=index):
                blocks[hop][rank * length : (rank + 1) * length, :] = pat_ref[index]

            digits = jnp.where(
                line == 0,
                row // DIGIT,
                jnp.where(
                    line == 1,
                    row % DIGIT,
                    jnp.where(line == 2, col // DIGIT, jnp.where(line == 3, col % DIGIT, 0)),
                ),
            )
            head = head + jnp.where((lane == rank) & valid, digits, 0)
        blocks[hop][capacity * length :, :] = head.astype(jnp.float32).astype(jnp.bfloat16)


def pack(patterns, tile_ids, rows, cols, tile_count, capacity):
    length = patterns.shape[-1]
    block = jax.ShapeDtypeStruct((capacity * length + HEAD, length), jnp.bfloat16)
    smem = pl.BlockSpec(memory_space=pltpu.SMEM)
    vmem = pl.BlockSpec(memory_space=pltpu.VMEM)
    return pl.pallas_call(
        functools.partial(pack_kernel, tile_count, capacity),
        out_shape=[block] * tile_count,
        in_specs=[smem, smem, smem, vmem],
        out_specs=[vmem] * tile_count,
        scratch_shapes=[
            pltpu.SMEM((tile_count,), jnp.int32),
            pltpu.SMEM((tile_count * capacity,), jnp.int32),
        ],
        compiler_params=pltpu.CompilerParams(vmem_limit_bytes=56 * 2**20),
        name="pack_patterns",
    )(tile_ids, rows, cols, patterns)


def prepare_kernel(object_hbm, probe_ref, chirp_ref, field, lit, sems):
    rows, columns = object_hbm.shape[1:]
    modes, _, length, _ = probe_ref.shape
    loads = [
        pltpu.make_async_copy(
            object_hbm.at[:, :, tile * LANES : (tile + 1) * LANES],
            field.at[:, tile, 0:rows, :],
            sems.at[tile],
        )
        for tile in range(columns // LANES)
    ]
    for load in loads:
        load.start()
    for mode in range(modes):
        for band in range(length // BAND):
            at = pl.ds(band * BAND, BAND)
            cr, ci = chirp_ref[0, at, :], chirp_ref[1, at, :]
            pr, pi = probe_ref[mode, 0, at, :], probe_ref[mode, 1, at, :]
            lit[mode, 0, at, :] = cr * pr - ci * pi
            lit[mode, 1, at, :] = cr * pi + ci * pr
    for load in loads:
        load.wait()


def prepare(object_field, probe, chirp):
    _, rows, columns = object_field.shape
    vmem = pl.BlockSpec(memory_space=pltpu.VMEM)
    return pl.pallas_call(
        prepare_kernel,
        out_shape=[
            jax.ShapeDtypeStruct((2, columns // LANES + 1, rows + 8, LANES), jnp.float32),
            jax.ShapeDtypeStruct(probe.shape, jnp.float32),
        ],
        in_specs=[pl.BlockSpec(memory_space=pl.ANY), vmem, vmem],
        out_specs=[vmem, vmem],
        scratch_shapes=[pltpu.SemaphoreType.DMA((columns // LANES,))],
        compiler_params=pltpu.CompilerParams(vmem_limit_bytes=16 * 2**20),
        name="prepare_strip",
    )(object_field, probe, chirp)


def step_kernel(block_count, capacity, scale, first, last, field, lit, dft_ref, chirp_ref, *rest):
    blocks = rest[:block_count]
    rest = rest[block_count:]
    if not first:
        total_before, grad_before = rest[:2]
        rest = rest[2:]
    total, grad = rest[:2]
    rest = rest[2:]
    if last:
        quarters = rest[:SQUARE]
        rest = rest[SQUARE:]
    (
        pats,
        heads,
        corners,
        list_row,
        list_col,
        list_pat,
        patch_even,
        patch_odd,
        wide,
        tall,
        in_sem,
        out_sem,
    ) = rest
    modes, _, length, _ = lit.shape
    column_tiles, rows = total.shape[1:3]
    block_rows = capacity * length + HEAD
    bands = length // BAND

    loads = [
        pltpu.make_async_copy(
            blocks[b], pats.at[b * block_rows : (b + 1) * block_rows], in_sem.at[b]
        )
        for b in range(block_count)
    ]
    for load in loads:
        load.start()

    def begin(index, carry):
        at = pl.ds(pl.multiple_of(index * 8, 8), 8)
        for plane in range(2):
            for tile in range(column_tiles):
                total[plane, tile, at, :] = (
                    jnp.zeros((8, LANES), jnp.float32)
                    if first
                    else total_before[plane, tile, at, :]
                )
        return carry

    lax.fori_loop(0, rows // 8, begin, 0)
    grad[...] = jnp.zeros_like(grad) if first else grad_before[...]

    for load in loads:
        load.wait()
    for b in range(block_count):
        heads[b * HEAD : (b + 1) * HEAD, :] = (
            pats[(b + 1) * block_rows - HEAD : (b + 1) * block_rows, :]
            .astype(jnp.float32)
            .astype(jnp.int32)
        )
    fetch = pltpu.make_async_copy(heads, corners, in_sem.at[block_count])
    fetch.start()
    fetch.wait()

    number = jnp.int32(0)
    for b in range(block_count):

        def note(rank, at, b=b):
            first_line = b * HEAD
            list_row[at] = corners[first_line, rank] * DIGIT + corners[first_line + 1, rank]
            list_col[at] = corners[first_line + 2, rank] * DIGIT + corners[first_line + 3, rank]
            list_pat[at] = b * block_rows + rank * length
            return at + 1

        number = lax.fori_loop(0, corners[b * HEAD + 4, 0], note, number)

    patch = (patch_even, patch_odd)
    group = BAND
    span = 4
    groups = length // group
    tall_rows = modes * group

    def item(index):
        index = jnp.clip(index, 0, number - 1)
        row, col = list_row[index], list_col[index]
        shift = col % LANES
        return row, col // LANES, shift, pl.multiple_of(list_pat[index], LANES)

    def exit_chunks(index, side):
        row, col, shift, _ = item(index)
        slot = (index >> 1) & 1
        back = (LANES - shift) % LANES

        def chunk(band):
            at = pl.ds(band * BAND, BAND)
            at_field = pl.ds(row + band * BAND, BAND)
            lane = lax.broadcasted_iota(jnp.int32, (BAND, LANES), 1)
            planes = []
            for plane in range(2):
                left = pltpu.roll(field[plane, col, at_field, :], back, 1)
                right = pltpu.roll(field[plane, col + 1, at_field, :], back, 1)
                cell = jnp.where(lane < LANES - shift, left, right)
                cell = cell.astype(jnp.bfloat16).astype(jnp.float32)
                patch[side][slot, plane, at, :] = cell
                planes.append(cell)
            pr, pi = planes
            for mode in range(modes):
                lr, li = lit[mode, 0, at, :], lit[mode, 1, at, :]
                lanes = pl.ds(mode * length, length)
                wide[side, at, lanes] = (lr * pr - li * pi).astype(jnp.bfloat16)
                wide[side, pl.ds(length + band * BAND, BAND), lanes] = (
                    lr * pi + li * pr
                ).astype(jnp.bfloat16)

        return [functools.partial(chunk, band) for band in range(bands)]

    def column_chunks(source, target, table):
        def chunk(mode):
            both = min(2, modes - mode)
            out = jnp.dot(
                dft_ref[table],
                wide[source, :, mode * length : (mode + both) * length],
                preferred_element_type=jnp.float32,
            ).astype(jnp.bfloat16)
            for q in range(both):
                for g in range(groups):
                    at = pl.ds(g * tall_rows + (mode + q) * group, group)
                    for plane in range(2):
                        tall[target, at, plane * length : (plane + 1) * length] = out[
                            plane * length + g * group : plane * length + (g + 1) * group,
                            q * length : (q + 1) * length,
                        ]

        return [functools.partial(chunk, mode) for mode in range(0, modes, 2)]

    def row_product(source, table, g):
        out = jnp.dot(
            tall[source, g * tall_rows : (g + span) * tall_rows, :],
            dft_ref[table],
            preferred_element_type=jnp.float32,
        )
        return [
            [
                tuple(
                    out[
                        k * tall_rows + mode * group : k * tall_rows + (mode + 1) * group,
                        plane * length : (plane + 1) * length,
                    ]
                    for plane in range(2)
                )
                for mode in range(modes)
            ]
            for k in range(span)
        ]

    def far_chunks(index, side):
        _, _, _, source = item(index)
        weight = jnp.where((index >= 0) & (index < number), jnp.float32(1.0), jnp.float32(0.0))

        def chunk(g):
            for k, waves in enumerate(row_product(side, 1, g)):
                amplitude(g + k, waves)

        def amplitude(g, waves):
            bright = None
            for fr, fi in waves:
                power = fr * fr + fi * fi
                bright = power if bright is None else bright + power
            measured = pats[pl.ds(source + g * group, group), :].astype(jnp.float32)
            inverse = jnp.minimum(lax.rsqrt(bright), 1.0 / AMP_FLOOR)
            factor = (measured * inverse - 1.0) * weight
            for mode in range(modes):
                fr, fi = waves[mode]
                lanes = pl.ds(mode * length, length)
                wide[2, pl.ds(g * group, group), lanes] = (fr * factor).astype(jnp.bfloat16)
                wide[2, pl.ds(length + g * group, group), lanes] = (fi * factor).astype(
                    jnp.bfloat16
                )

        return [functools.partial(chunk, g) for g in range(0, groups, span)]

    def step_chunks(index, side):
        row, col, shift, _ = item(index)
        slot = (index >> 1) & 1

        def chunk(g):
            for k, waves in enumerate(row_product(2 + side, 0, g)):
                update(g + k, waves)

        def update(g, waves):
            at = pl.ds(g * group, group)
            at_field = pl.ds(row + g * group, group)
            lane = lax.broadcasted_iota(jnp.int32, (group, LANES), 1)
            pr, pi = patch[side][slot, 0, at, :], patch[side][slot, 1, at, :]
            steps = [None, None]
            for mode in range(modes):
                at_gr = pl.ds((2 * mode) * length + g * group, group)
                at_gi = pl.ds((2 * mode + 1) * length + g * group, group)
                lr, li = lit[mode, 0, at, :], lit[mode, 1, at, :]
                nr, ni = waves[mode]
                sr, si = lr * nr + li * ni, lr * ni - li * nr
                steps = [sr, si] if mode == 0 else [steps[0] + sr, steps[1] + si]
                grad[at_gr, :] += pr * nr + pi * ni
                grad[at_gi, :] += pr * ni - pi * nr
            places = [(plane, col + tile) for plane in range(2) for tile in range(2)]
            olds = [total[plane, tile, at_field, :] for plane, tile in places]
            sums = []
            for plane in range(2):
                moved = steps[plane].astype(jnp.bfloat16).astype(jnp.float32)
                moved = pltpu.roll(moved, shift, 1)
                sums.append(olds[2 * plane] + jnp.where(lane >= shift, moved, 0.0))
                sums.append(olds[2 * plane + 1] + jnp.where(lane < shift, moved, 0.0))
            for (plane, tile), value in zip(places, sums):
                total[plane, tile, at_field, :] = value

        return [functools.partial(chunk, g) for g in range(0, groups, span)]

    def run(*lists):
        order = []
        for rank, chunks in enumerate(lists):
            order += [((n + 0.5) / len(chunks), rank, chunk) for n, chunk in enumerate(chunks)]
        for _, _, chunk in sorted(order, key=lambda entry: entry[:2]):
            chunk()

    def visit(turn, carry):
        for side in range(2):
            at, other = 2 * turn + side, 1 - side
            run(far_chunks(at, side))
            run(column_chunks(other, other, 0), exit_chunks(at + 2, side))
            run(column_chunks(2, 2 + side, 1), step_chunks(at - 1, other))
        return carry

    @pl.when(number > 0)
    def _():
        tall[3] = jnp.zeros(tall.shape[1:], tall.dtype)
        patch[1][1] = jnp.zeros(patch[1].shape[1:], jnp.float32)
        run(exit_chunks(jnp.int32(0), 0))
        run(column_chunks(0, 0, 0), exit_chunks(jnp.int32(1), 1))
        lax.fori_loop(0, number // 2 + 1, visit, 0)

    if not last:
        return
    for mode in range(modes):
        for band in range(bands):
            at = pl.ds(band * BAND, BAND)
            at_gr = pl.ds((2 * mode) * length + band * BAND, BAND)
            at_gi = pl.ds((2 * mode + 1) * length + band * BAND, BAND)
            cr, ci = chirp_ref[0, at, :] * scale, chirp_ref[1, at, :] * scale
            gr, gi = grad[at_gr, :], grad[at_gi, :]
            grad[at_gr, :] = cr * gr + ci * gi
            grad[at_gi, :] = cr * gi - ci * gr
    pos = lax.axis_index("pos")
    me = lax.axis_index("tile") % (SQUARE // 2) * 2 + pos
    quarter = grad.shape[0] // SQUARE
    parts = [
        (grad.at[pl.ds(pl.multiple_of((me ^ turn) * quarter, 8), quarter), :], outside)
        for turn, outside in enumerate(quarters)
    ]
    stores = [
        pltpu.make_async_copy(inside, outside, out_sem.at[n])
        for n, (inside, outside) in enumerate(parts)
    ]
    for store in stores:
        store.start()
    for store in stores:
        store.wait()


def step(field, lit, blocks, tables, scale, capacity, before, last):
    modes, _, length, _ = lit.shape
    column_tiles, rows = field.shape[1:3]
    count = len(blocks)
    slots = count * capacity
    vmem = pl.BlockSpec(memory_space=pltpu.VMEM)
    hbm = pl.BlockSpec(memory_space=pl.ANY)
    f32, bf16 = jnp.float32, jnp.bfloat16
    outs = [
        jax.ShapeDtypeStruct(field.shape, f32),
        jax.ShapeDtypeStruct((2 * modes * length, length), f32),
    ]
    specs = [vmem, vmem]
    if last:
        outs += [jax.ShapeDtypeStruct((2 * modes * length // SQUARE, length), f32)] * SQUARE
        specs += [hbm] * SQUARE
    return pl.pallas_call(
        functools.partial(step_kernel, count, capacity, scale, not before, last),
        out_shape=outs,
        in_specs=[vmem] * 4 + [hbm] * count + [vmem] * len(before),
        out_specs=specs,
        scratch_shapes=[
            pltpu.VMEM((count * (capacity * length + HEAD), length), bf16),
            pltpu.VMEM((count * HEAD, LANES), jnp.int32),
            pltpu.SMEM((count * HEAD, LANES), jnp.int32),
            pltpu.SMEM((slots,), jnp.int32),
            pltpu.SMEM((slots,), jnp.int32),
            pltpu.SMEM((slots,), jnp.int32),
            pltpu.VMEM((2, 2, length, length), f32),
            pltpu.VMEM((2, 2, length, length), f32),
            pltpu.VMEM((3, 2 * length, modes * length), bf16),
            pltpu.VMEM((4, modes * length, 2 * length), bf16),
            pltpu.SemaphoreType.DMA((count + 1,)),
            pltpu.SemaphoreType.DMA((SQUARE,)),
        ],
        compiler_params=pltpu.CompilerParams(vmem_limit_bytes=26 * 2**20),
        cost_estimate=pl.CostEstimate(
            flops=slots * modes * 4 * 8 * length**3,
            bytes_accessed=16 * 2**20,
            transcendentals=slots * length**2,
        ),
        name="gradient_step",
    )(field, lit, *tables, *blocks, *before)


def give_kernel(total, send, sems):
    half = send.shape[2] // LANES
    side = 1 - lax.axis_index("pos")
    stores = [
        pltpu.make_async_copy(
            total.at[:, side * half + tile, 0 : send.shape[1], :],
            send.at[:, :, tile * LANES : (tile + 1) * LANES],
            sems.at[tile],
        )
        for tile in range(half)
    ]
    for store in stores:
        store.start()
    for store in stores:
        store.wait()


def finish_kernel(total, received, out):
    half = out.shape[2] // LANES
    side = lax.axis_index("pos")

    def add(index, carry):
        at = pl.ds(pl.multiple_of(index * 8, 8), 8)
        for plane in range(2):
            for tile in range(half):
                lanes = pl.ds(tile * LANES, LANES)
                out[plane, at, lanes] = (
                    total[plane, side * half + tile, at, :] + received[plane, at, lanes]
                )
        return carry

    lax.fori_loop(0, out.shape[1] // 8, add, 0)


def halves(total, received=None):
    _, column_tiles, rows, _ = total.shape
    half = (column_tiles - 1) // 2
    shape = jax.ShapeDtypeStruct((2, rows - 8, half * LANES), jnp.float32)
    vmem = pl.BlockSpec(memory_space=pltpu.VMEM)
    cost = pl.CostEstimate(flops=2**20, bytes_accessed=4 * 2**20, transcendentals=0)
    limit = pltpu.CompilerParams(vmem_limit_bytes=16 * 2**20)
    if received is None:
        return pl.pallas_call(
            give_kernel,
            out_shape=shape,
            in_specs=[vmem],
            out_specs=pl.BlockSpec(memory_space=pl.ANY),
            scratch_shapes=[pltpu.SemaphoreType.DMA((half,))],
            compiler_params=limit,
            cost_estimate=cost,
            name="give_half",
        )(total)
    return pl.pallas_call(
        finish_kernel,
        out_shape=shape,
        in_specs=[vmem, vmem],
        out_specs=vmem,
        compiler_params=limit,
        cost_estimate=cost,
        name="add_half",
    )(total, received)


def from_peer(array, turn, devices):
    pairs = [(i, i ^ turn) for i in range(devices)]
    return lax.ppermute(array, ("tile", "pos"), pairs)


def tree_sum(parts):
    while len(parts) > 1:
        parts = [a + b for a, b in zip(parts[::2], parts[1::2])]
    return parts[0]


def on_device(object_field, probe, patterns, scan_tile, scan_row, scan_col):
    tile_count = lax.axis_size("tile")
    pos_count = lax.axis_size("pos")
    number, length = patterns.shape[0], patterns.shape[-1]
    capacity = max(2, 2 * number // tile_count)
    scale = 1.0 / math.sqrt(number * tile_count * pos_count)
    tables = (jnp.asarray(dft_tables(length)), jnp.asarray(chirp_table(length)))
    blocks = pack(patterns, scan_tile[:, 0], scan_row, scan_col, tile_count, capacity)
    field, lit = prepare(object_field, probe, tables[1])
    late = tile_count * 3 // 4
    order = [*range(late - tile_count // 4), *range(late, tile_count), *range(tile_count // 2, late)]
    arrived = [blocks[0]]
    for hop in order[1:]:
        block = blocks[hop]
        if len(arrived) >= late:
            block = lax.optimization_barrier((block, arrived[1], lit))[0]
        arrived.append(lax.ppermute(block, "tile", [(i, i ^ hop) for i in range(tile_count)]))
    cuts = [0, tile_count // 2, tile_count * 3 // 4, tile_count]
    sums = ()
    for a, b in zip(cuts[:-1], cuts[1:]):
        sums = step(field, lit, arrived[a:b], tables, scale, capacity, sums, b == tile_count)
    total, grads = sums[0], sums[2:]

    devices = tile_count * pos_count
    inside, across = range(1, SQUARE), range(SQUARE, devices, SQUARE)
    part = tree_sum([grads[0]] + [from_peer(grads[turn], turn, devices) for turn in inside])
    send, part = lax.optimization_barrier((halves(total), part))
    object_step = halves(total, lax.ppermute(send, "pos", [(0, 1), (1, 0)]))
    part = tree_sum(
        [part]
        + [from_peer(part, turn, devices) for turn in across]
    )
    part, object_step = lax.optimization_barrier((part, object_step))
    square = [part] + [from_peer(part, turn, devices) for turn in inside]
    me = lax.axis_index(("tile", "pos"))
    for bit in (1, 2):
        swapped = (me & bit) != 0
        square = [jnp.where(swapped, square[q ^ bit], square[q]) for q in range(SQUARE)]
    return (object_step, jnp.concatenate(square).reshape(probe.shape))


def solution(mesh):
    placed = (
        P("groups", "tile", None),
        P("groups", None, None, None),
        P(("groups", "tile", "pos"), None, None),
        P(("groups", "tile", "pos"), None),
        P(("groups", "tile", "pos")),
        P(("groups", "tile", "pos")),
    )
    return jax.shard_map(
        on_device,
        mesh=mesh,
        in_specs=placed,
        out_specs=(P("groups", "tile", "pos"), P("groups", None, None, None)),
        check_vma=False,
    )
```

```python
import functools
import math

import jax
import jax.numpy as jnp
import numpy as np
from jax import lax
from jax.experimental import pallas as pl
from jax.experimental.pallas import tpu as pltpu
from jax.sharding import PartitionSpec as P

AMP_FLOOR = 0.5
HEAD = 16
DIGIT = 16
LANES = 128
SQUARE = 4

BAND = 16


def dft_tables(length):
    indices = np.arange(length, dtype=np.int32)
    products = indices[:, None] * indices[None, :] % length
    angles = products.astype(np.float32) * np.float32(-2.0 * math.pi / length)
    factor = np.float32(1.0 / math.sqrt(length))
    real = (np.cos(angles) * factor).astype(jnp.bfloat16)
    imag = (np.sin(angles) * factor).astype(jnp.bfloat16)
    forward = np.block([[real, -imag], [imag, real]])
    backward = np.block([[real, imag], [-imag, real]])
    return np.stack([forward, backward])


def chirp_table(length):
    offsets = np.arange(length, dtype=np.int32) - length // 2
    squares = offsets * offsets
    phases = (squares[:, None] + squares[None, :]).astype(np.float32) * np.float32(
        0.5 * math.pi / length
    )
    return np.stack([np.cos(phases), np.sin(phases)]).astype(np.float32)


def pack_kernel(tile_count, capacity, tile_ref, row_ref, col_ref, pat_ref, *rest):
    blocks, count_ref, source_ref = rest[:tile_count], rest[tile_count], rest[tile_count + 1]
    number, length = pat_ref.shape[0], pat_ref.shape[1]
    me = lax.axis_index("tile")
    for hop in range(tile_count):
        count_ref[hop] = 0

    def place(index, carry):
        hop = tile_ref[index] ^ me
        rank = count_ref[hop]
        count_ref[hop] = rank + 1
        source_ref[hop * capacity + rank] = index
        return carry

    lax.fori_loop(0, number, place, 0)
    lane = lax.broadcasted_iota(jnp.int32, (HEAD, LANES), 1)
    line = lax.broadcasted_iota(jnp.int32, (HEAD, LANES), 0)
    for hop in range(tile_count):
        count = count_ref[hop]
        corner = jnp.zeros((HEAD, LANES), jnp.int32)
        for rank in range(capacity):
            valid = rank < count
            index = jnp.where(valid, source_ref[hop * capacity + rank], 0)
            value = jnp.where(line < 2, row_ref[index], col_ref[index])
            corner = jnp.where((lane == rank) & valid, value, corner)

            @pl.when(valid)
            def _(hop=hop, rank=rank, index=index):
                blocks[hop][rank * length : (rank + 1) * length, :] = pat_ref[index]

        digits = jnp.where(line % 2 == 0, corner // DIGIT, corner % DIGIT)
        digits = jnp.where(line < 4, digits, jnp.where(line == 4, count, 0))
        blocks[hop][capacity * length :, :] = digits.astype(jnp.float32).astype(jnp.bfloat16)


def pack(patterns, tile_ids, rows, cols, tile_count, capacity):
    length = patterns.shape[-1]
    block = jax.ShapeDtypeStruct((capacity * length + HEAD, length), jnp.bfloat16)
    smem = pl.BlockSpec(memory_space=pltpu.SMEM)
    vmem = pl.BlockSpec(memory_space=pltpu.VMEM)
    return pl.pallas_call(
        functools.partial(pack_kernel, tile_count, capacity),
        out_shape=[block] * tile_count,
        in_specs=[smem, smem, smem, vmem],
        out_specs=[vmem] * tile_count,
        scratch_shapes=[
            pltpu.SMEM((tile_count,), jnp.int32),
            pltpu.SMEM((tile_count * capacity,), jnp.int32),
        ],
        compiler_params=pltpu.CompilerParams(vmem_limit_bytes=56 * 2**20),
        name="pack_patterns",
    )(tile_ids, rows, cols, patterns)


def prepare_kernel(object_hbm, probe_ref, chirp_ref, field, lit, sems):
    rows, columns = object_hbm.shape[1:]
    modes, _, length, _ = probe_ref.shape
    loads = [
        pltpu.make_async_copy(
            object_hbm.at[:, :, tile * LANES : (tile + 1) * LANES],
            field.at[:, tile, 0:rows, :],
            sems.at[tile],
        )
        for tile in range(columns // LANES)
    ]
    for load in loads:
        load.start()
    for mode in range(modes):
        for band in range(length // BAND):
            at = pl.ds(band * BAND, BAND)
            cr, ci = chirp_ref[0, at, :], chirp_ref[1, at, :]
            pr, pi = probe_ref[mode, 0, at, :], probe_ref[mode, 1, at, :]
            lit[mode, 0, at, :] = cr * pr - ci * pi
            lit[mode, 1, at, :] = cr * pi + ci * pr
    for load in loads:
        load.wait()


def prepare(object_field, probe, chirp):
    _, rows, columns = object_field.shape
    vmem = pl.BlockSpec(memory_space=pltpu.VMEM)
    return pl.pallas_call(
        prepare_kernel,
        out_shape=[
            jax.ShapeDtypeStruct((2, columns // LANES + 1, rows + 8, LANES), jnp.float32),
            jax.ShapeDtypeStruct(probe.shape, jnp.float32),
        ],
        in_specs=[pl.BlockSpec(memory_space=pl.ANY), vmem, vmem],
        out_specs=[vmem, vmem],
        scratch_shapes=[pltpu.SemaphoreType.DMA((columns // LANES,))],
        compiler_params=pltpu.CompilerParams(vmem_limit_bytes=16 * 2**20),
        name="prepare_strip",
    )(object_field, probe, chirp)


def step_kernel(block_count, capacity, scale, first, last, field, lit, dft_ref, chirp_ref, *rest):
    blocks = rest[:block_count]
    rest = rest[block_count:]
    if not first:
        total_before, grad_before = rest[:2]
        rest = rest[2:]
    total, grad = rest[:2]
    rest = rest[2:]
    if last:
        quarters = rest[:SQUARE]
        rest = rest[SQUARE:]
    (
        pats,
        heads,
        corners,
        list_row,
        list_col,
        list_pat,
        patch_even,
        patch_odd,
        wide,
        tall,
        in_sem,
        out_sem,
    ) = rest
    modes, _, length, _ = lit.shape
    column_tiles, rows = total.shape[1:3]
    block_rows = capacity * length + HEAD
    bands = length // BAND

    loads = [
        pltpu.make_async_copy(
            blocks[b], pats.at[b * block_rows : (b + 1) * block_rows], in_sem.at[b]
        )
        for b in range(block_count)
    ]
    for load in loads:
        load.start()

    def begin(index, carry):
        at = pl.ds(pl.multiple_of(index * 8, 8), 8)
        for plane in range(2):
            for tile in range(column_tiles):
                total[plane, tile, at, :] = (
                    jnp.zeros((8, LANES), jnp.float32)
                    if first
                    else total_before[plane, tile, at, :]
                )
        return carry

    lax.fori_loop(0, rows // 8, begin, 0)
    grad[...] = jnp.zeros_like(grad) if first else grad_before[...]

    for load in loads:
        load.wait()
    for b in range(block_count):
        heads[b * HEAD : (b + 1) * HEAD, :] = (
            pats[(b + 1) * block_rows - HEAD : (b + 1) * block_rows, :]
            .astype(jnp.float32)
            .astype(jnp.int32)
        )
    fetch = pltpu.make_async_copy(heads, corners, in_sem.at[block_count])
    fetch.start()
    fetch.wait()

    number = jnp.int32(0)
    for b in range(block_count):

        def note(rank, at, b=b):
            first_line = b * HEAD
            list_row[at] = corners[first_line, rank] * DIGIT + corners[first_line + 1, rank]
            list_col[at] = corners[first_line + 2, rank] * DIGIT + corners[first_line + 3, rank]
            list_pat[at] = b * block_rows + rank * length
            return at + 1

        number = lax.fori_loop(0, corners[b * HEAD + 4, 0], note, number)

    patch = (patch_even, patch_odd)
    group = BAND
    span = 4
    groups = length // group
    tall_rows = modes * group

    def item(index):
        index = jnp.clip(index, 0, number - 1)
        row, col = list_row[index], list_col[index]
        shift = col % LANES
        return row, col // LANES, shift, pl.multiple_of(list_pat[index], LANES)

    def exit_chunks(index, side):
        row, col, shift, _ = item(index)
        slot = (index >> 1) & 1
        back = (LANES - shift) % LANES

        def chunk(band):
            at = pl.ds(band * BAND, BAND)
            at_field = pl.ds(row + band * BAND, BAND)
            lane = lax.broadcasted_iota(jnp.int32, (BAND, LANES), 1)
            planes = []
            for plane in range(2):
                left = pltpu.roll(field[plane, col, at_field, :], back, 1)
                right = pltpu.roll(field[plane, col + 1, at_field, :], back, 1)
                cell = jnp.where(lane < LANES - shift, left, right)
                cell = cell.astype(jnp.bfloat16).astype(jnp.float32)
                patch[side][slot, plane, at, :] = cell
                planes.append(cell)
            pr, pi = planes
            for mode in range(modes):
                lr, li = lit[mode, 0, at, :], lit[mode, 1, at, :]
                lanes = pl.ds(mode * length, length)
                wide[side, at, lanes] = (lr * pr - li * pi).astype(jnp.bfloat16)
                wide[side, pl.ds(length + band * BAND, BAND), lanes] = (
                    lr * pi + li * pr
                ).astype(jnp.bfloat16)

        return [functools.partial(chunk, band) for band in range(bands)]

    def column_chunks(source, target, table):
        def chunk(mode):
            both = min(2, modes - mode)
            out = jnp.dot(
                dft_ref[table],
                wide[source, :, mode * length : (mode + both) * length],
                preferred_element_type=jnp.float32,
            ).astype(jnp.bfloat16)
            for q in range(both):
                for g in range(groups):
                    at = pl.ds(g * tall_rows + (mode + q) * group, group)
                    for plane in range(2):
                        tall[target, at, plane * length : (plane + 1) * length] = out[
                            plane * length + g * group : plane * length + (g + 1) * group,
                            q * length : (q + 1) * length,
                        ]

        return [functools.partial(chunk, mode) for mode in range(0, modes, 2)]

    def row_product(source, table, g):
        out = jnp.dot(
            tall[source, g * tall_rows : (g + span) * tall_rows, :],
            dft_ref[table],
            preferred_element_type=jnp.float32,
        )
        return [
            [
                tuple(
                    out[
                        k * tall_rows + mode * group : k * tall_rows + (mode + 1) * group,
                        plane * length : (plane + 1) * length,
                    ]
                    for plane in range(2)
                )
                for mode in range(modes)
            ]
            for k in range(span)
        ]

    def far_chunks(index, side):
        _, _, _, source = item(index)
        weight = jnp.where((index >= 0) & (index < number), jnp.float32(1.0), jnp.float32(0.0))

        def chunk(g):
            for k, waves in enumerate(row_product(side, 1, g)):
                amplitude(g + k, waves)

        def amplitude(g, waves):
            bright = None
            for fr, fi in waves:
                power = fr * fr + fi * fi
                bright = power if bright is None else bright + power
            measured = pats[pl.ds(source + g * group, group), :].astype(jnp.float32)
            inverse = jnp.minimum(lax.rsqrt(bright), 1.0 / AMP_FLOOR)
            factor = (measured * inverse - 1.0) * weight
            for mode in range(modes):
                fr, fi = waves[mode]
                lanes = pl.ds(mode * length, length)
                wide[2, pl.ds(g * group, group), lanes] = (fr * factor).astype(jnp.bfloat16)
                wide[2, pl.ds(length + g * group, group), lanes] = (fi * factor).astype(
                    jnp.bfloat16
                )

        return [functools.partial(chunk, g) for g in range(0, groups, span)]

    def step_chunks(index, side):
        row, col, shift, _ = item(index)
        slot = (index >> 1) & 1

        def chunk(g):
            for k, waves in enumerate(row_product(2 + side, 0, g)):
                update(g + k, waves)

        def update(g, waves):
            at = pl.ds(g * group, group)
            at_field = pl.ds(row + g * group, group)
            lane = lax.broadcasted_iota(jnp.int32, (group, LANES), 1)
            pr, pi = patch[side][slot, 0, at, :], patch[side][slot, 1, at, :]
            steps = [None, None]
            for mode in range(modes):
                at_gr = pl.ds((2 * mode) * length + g * group, group)
                at_gi = pl.ds((2 * mode + 1) * length + g * group, group)
                lr, li = lit[mode, 0, at, :], lit[mode, 1, at, :]
                nr, ni = waves[mode]
                sr, si = lr * nr + li * ni, lr * ni - li * nr
                steps = [sr, si] if mode == 0 else [steps[0] + sr, steps[1] + si]
                grad[at_gr, :] += pr * nr + pi * ni
                grad[at_gi, :] += pr * ni - pi * nr
            places = [(plane, col + tile) for plane in range(2) for tile in range(2)]
            olds = [total[plane, tile, at_field, :] for plane, tile in places]
            sums = []
            for plane in range(2):
                moved = steps[plane].astype(jnp.bfloat16).astype(jnp.float32)
                moved = pltpu.roll(moved, shift, 1)
                sums.append(olds[2 * plane] + jnp.where(lane >= shift, moved, 0.0))
                sums.append(olds[2 * plane + 1] + jnp.where(lane < shift, moved, 0.0))
            for (plane, tile), value in zip(places, sums):
                total[plane, tile, at_field, :] = value

        return [functools.partial(chunk, g) for g in range(0, groups, span)]

    def run(*lists):
        order = []
        for rank, chunks in enumerate(lists):
            order += [((n + 0.5) / len(chunks), rank, chunk) for n, chunk in enumerate(chunks)]
        for _, _, chunk in sorted(order, key=lambda entry: entry[:2]):
            chunk()

    def visit(turn, carry):
        for side in range(2):
            at, other = 2 * turn + side, 1 - side
            run(far_chunks(at, side))
            run(column_chunks(other, other, 0), exit_chunks(at + 2, side))
            run(column_chunks(2, 2 + side, 1), step_chunks(at - 1, other))
        return carry

    @pl.when(number > 0)
    def _():
        tall[3] = jnp.zeros(tall.shape[1:], tall.dtype)
        patch[1][1] = jnp.zeros(patch[1].shape[1:], jnp.float32)
        run(exit_chunks(jnp.int32(0), 0))
        run(column_chunks(0, 0, 0), exit_chunks(jnp.int32(1), 1))
        lax.fori_loop(0, (number + 1) // 2, visit, 0)

        @pl.when(number % 2 == 0)
        def _():
            run(step_chunks(number - 1, 1))

    if not last:
        return
    for mode in range(modes):
        for band in range(bands):
            at = pl.ds(band * BAND, BAND)
            at_gr = pl.ds((2 * mode) * length + band * BAND, BAND)
            at_gi = pl.ds((2 * mode + 1) * length + band * BAND, BAND)
            cr, ci = chirp_ref[0, at, :] * scale, chirp_ref[1, at, :] * scale
            gr, gi = grad[at_gr, :], grad[at_gi, :]
            grad[at_gr, :] = cr * gr + ci * gi
            grad[at_gi, :] = cr * gi - ci * gr
    pos = lax.axis_index("pos")
    me = lax.axis_index("tile") % (SQUARE // 2) * 2 + pos
    quarter = grad.shape[0] // SQUARE
    parts = [
        (grad.at[pl.ds(pl.multiple_of((me ^ turn) * quarter, 8), quarter), :], outside)
        for turn, outside in enumerate(quarters)
    ]
    stores = [
        pltpu.make_async_copy(inside, outside, out_sem.at[n])
        for n, (inside, outside) in enumerate(parts)
    ]
    for store in stores:
        store.start()
    for store in stores:
        store.wait()


def step(field, lit, blocks, tables, scale, capacity, before, last):
    modes, _, length, _ = lit.shape
    column_tiles, rows = field.shape[1:3]
    count = len(blocks)
    slots = count * capacity
    vmem = pl.BlockSpec(memory_space=pltpu.VMEM)
    hbm = pl.BlockSpec(memory_space=pl.ANY)
    f32, bf16 = jnp.float32, jnp.bfloat16
    outs = [
        jax.ShapeDtypeStruct(field.shape, f32),
        jax.ShapeDtypeStruct((2 * modes * length, length), f32),
    ]
    specs = [vmem, vmem]
    if last:
        outs += [jax.ShapeDtypeStruct((2 * modes * length // SQUARE, length), f32)] * SQUARE
        specs += [hbm] * SQUARE
    return pl.pallas_call(
        functools.partial(step_kernel, count, capacity, scale, not before, last),
        out_shape=outs,
        in_specs=[vmem] * 4 + [hbm] * count + [vmem] * len(before),
        out_specs=specs,
        scratch_shapes=[
            pltpu.VMEM((count * (capacity * length + HEAD), length), bf16),
            pltpu.VMEM((count * HEAD, LANES), jnp.int32),
            pltpu.SMEM((count * HEAD, LANES), jnp.int32),
            pltpu.SMEM((slots,), jnp.int32),
            pltpu.SMEM((slots,), jnp.int32),
            pltpu.SMEM((slots,), jnp.int32),
            pltpu.VMEM((2, 2, length, length), f32),
            pltpu.VMEM((2, 2, length, length), f32),
            pltpu.VMEM((3, 2 * length, modes * length), bf16),
            pltpu.VMEM((4, modes * length, 2 * length), bf16),
            pltpu.SemaphoreType.DMA((count + 1,)),
            pltpu.SemaphoreType.DMA((SQUARE,)),
        ],
        compiler_params=pltpu.CompilerParams(vmem_limit_bytes=26 * 2**20),
        cost_estimate=pl.CostEstimate(
            flops=slots * modes * 4 * 8 * length**3,
            bytes_accessed=16 * 2**20,
            transcendentals=slots * length**2,
        ),
        name="gradient_step",
    )(field, lit, *tables, *blocks, *before)


def give_kernel(total, send, sems):
    half = send.shape[2] // LANES
    side = 1 - lax.axis_index("pos")
    stores = [
        pltpu.make_async_copy(
            total.at[:, side * half + tile, 0 : send.shape[1], :],
            send.at[:, :, tile * LANES : (tile + 1) * LANES],
            sems.at[tile],
        )
        for tile in range(half)
    ]
    for store in stores:
        store.start()
    for store in stores:
        store.wait()


def finish_kernel(total, received, out):
    half = out.shape[2] // LANES
    side = lax.axis_index("pos")

    def add(index, carry):
        at = pl.ds(pl.multiple_of(index * 8, 8), 8)
        for plane in range(2):
            for tile in range(half):
                lanes = pl.ds(tile * LANES, LANES)
                out[plane, at, lanes] = (
                    total[plane, side * half + tile, at, :] + received[plane, at, lanes]
                )
        return carry

    lax.fori_loop(0, out.shape[1] // 8, add, 0)


def halves(total, received=None):
    _, column_tiles, rows, _ = total.shape
    half = (column_tiles - 1) // 2
    shape = jax.ShapeDtypeStruct((2, rows - 8, half * LANES), jnp.float32)
    vmem = pl.BlockSpec(memory_space=pltpu.VMEM)
    cost = pl.CostEstimate(flops=2**20, bytes_accessed=4 * 2**20, transcendentals=0)
    limit = pltpu.CompilerParams(vmem_limit_bytes=16 * 2**20)
    if received is None:
        return pl.pallas_call(
            give_kernel,
            out_shape=shape,
            in_specs=[vmem],
            out_specs=pl.BlockSpec(memory_space=pl.ANY),
            scratch_shapes=[pltpu.SemaphoreType.DMA((half,))],
            compiler_params=limit,
            cost_estimate=cost,
            name="give_half",
        )(total)
    return pl.pallas_call(
        finish_kernel,
        out_shape=shape,
        in_specs=[vmem, vmem],
        out_specs=vmem,
        compiler_params=limit,
        cost_estimate=cost,
        name="add_half",
    )(total, received)


def from_peer(array, turn, devices):
    pairs = [(i, i ^ turn) for i in range(devices)]
    return lax.ppermute(array, ("tile", "pos"), pairs)


def tree_sum(parts):
    while len(parts) > 1:
        parts = [a + b for a, b in zip(parts[::2], parts[1::2])]
    return parts[0]


def on_device(object_field, probe, patterns, scan_tile, scan_row, scan_col):
    tile_count = lax.axis_size("tile")
    pos_count = lax.axis_size("pos")
    number, length = patterns.shape[0], patterns.shape[-1]
    capacity = max(2, 2 * number // tile_count)
    scale = 1.0 / math.sqrt(number * tile_count * pos_count)
    tables = (jnp.asarray(dft_tables(length)), jnp.asarray(chirp_table(length)))
    blocks = pack(patterns, scan_tile[:, 0], scan_row, scan_col, tile_count, capacity)
    field, lit = prepare(object_field, probe, tables[1])
    late = tile_count * 3 // 4
    order = [*range(late - tile_count // 4), *range(late, tile_count), *range(tile_count // 2, late)]
    arrived = [blocks[0]]
    for hop in order[1:]:
        block = blocks[hop]
        if len(arrived) >= late:
            block = lax.optimization_barrier((block, arrived[1], lit))[0]
        arrived.append(lax.ppermute(block, "tile", [(i, i ^ hop) for i in range(tile_count)]))
    cuts = [0, tile_count // 2, tile_count * 3 // 4, tile_count]
    sums = ()
    for a, b in zip(cuts[:-1], cuts[1:]):
        sums = step(field, lit, arrived[a:b], tables, scale, capacity, sums, b == tile_count)
    total, grads = sums[0], sums[2:]

    devices = tile_count * pos_count
    inside, across = range(1, SQUARE), range(SQUARE, devices, SQUARE)
    part = tree_sum([grads[0]] + [from_peer(grads[turn], turn, devices) for turn in inside])
    send, part = lax.optimization_barrier((halves(total), part))
    object_step = halves(total, lax.ppermute(send, "pos", [(0, 1), (1, 0)]))
    received = [from_peer(part, turn, devices) for turn in across]
    object_step, *received = lax.optimization_barrier([object_step] + received)
    part = tree_sum([part] + received)
    square = [part] + [from_peer(part, turn, devices) for turn in inside]
    me = lax.axis_index(("tile", "pos"))
    for bit in (1, 2):
        swapped = (me & bit) != 0
        square = [jnp.where(swapped, square[q ^ bit], square[q]) for q in range(SQUARE)]
    return (object_step, jnp.concatenate(square).reshape(probe.shape))


def solution(mesh):
    placed = (
        P("groups", "tile", None),
        P("groups", None, None, None),
        P(("groups", "tile", "pos"), None, None),
        P(("groups", "tile", "pos"), None),
        P(("groups", "tile", "pos")),
        P(("groups", "tile", "pos")),
    )
    return jax.shard_map(
        on_device,
        mesh=mesh,
        in_specs=placed,
        out_specs=(P("groups", "tile", "pos"), P("groups", None, None, None)),
        check_vma=False,
    )
```

```python
import functools
import math

import jax
import jax.numpy as jnp
import numpy as np
from jax import lax
from jax.experimental import pallas as pl
from jax.experimental.pallas import tpu as pltpu
from jax.sharding import PartitionSpec as P

AMP_FLOOR = 0.5
HEAD = 16
DIGIT = 16
LANES = 128
SQUARE = 4

BAND = 16


def dft_tables(length):
    indices = np.arange(length, dtype=np.int32)
    products = indices[:, None] * indices[None, :] % length
    angles = products.astype(np.float32) * np.float32(-2.0 * math.pi / length)
    factor = np.float32(1.0 / math.sqrt(length))
    real = (np.cos(angles) * factor).astype(jnp.bfloat16)
    imag = (np.sin(angles) * factor).astype(jnp.bfloat16)
    forward = np.block([[real, -imag], [imag, real]])
    backward = np.block([[real, imag], [-imag, real]])
    return np.stack([forward, backward])


def chirp_table(length):
    offsets = np.arange(length, dtype=np.int32) - length // 2
    squares = offsets * offsets
    phases = (squares[:, None] + squares[None, :]).astype(np.float32) * np.float32(
        0.5 * math.pi / length
    )
    return np.stack([np.cos(phases), np.sin(phases)]).astype(np.float32)


def pack_kernel(tile_count, capacity, tile_ref, row_ref, col_ref, pat_ref, *rest):
    blocks, count_ref, source_ref = rest[:tile_count], rest[tile_count], rest[tile_count + 1]
    number, length = pat_ref.shape[0], pat_ref.shape[1]
    me = lax.axis_index("tile")
    for hop in range(tile_count):
        count_ref[hop] = 0

    def place(index, carry):
        hop = tile_ref[index] ^ me
        rank = count_ref[hop]
        count_ref[hop] = rank + 1
        source_ref[hop * capacity + rank] = index
        return carry

    lax.fori_loop(0, number, place, 0)
    lane = lax.broadcasted_iota(jnp.int32, (HEAD, LANES), 1)
    line = lax.broadcasted_iota(jnp.int32, (HEAD, LANES), 0)
    for hop in range(tile_count):
        count = count_ref[hop]
        corner = jnp.zeros((HEAD, LANES), jnp.int32)
        for rank in range(capacity):
            valid = rank < count
            index = jnp.where(valid, source_ref[hop * capacity + rank], 0)
            value = jnp.where(line < 2, row_ref[index], col_ref[index])
            corner = jnp.where((lane == rank) & valid, value, corner)

            @pl.when(valid)
            def _(hop=hop, rank=rank, index=index):
                blocks[hop][rank * length : (rank + 1) * length, :] = pat_ref[index]

        digits = jnp.where(line % 2 == 0, corner // DIGIT, corner % DIGIT)
        digits = jnp.where(line < 4, digits, jnp.where(line == 4, count, 0))
        blocks[hop][capacity * length :, :] = digits.astype(jnp.float32).astype(jnp.bfloat16)


def pack(patterns, tile_ids, rows, cols, tile_count, capacity):
    length = patterns.shape[-1]
    block = jax.ShapeDtypeStruct((capacity * length + HEAD, length), jnp.bfloat16)
    smem = pl.BlockSpec(memory_space=pltpu.SMEM)
    vmem = pl.BlockSpec(memory_space=pltpu.VMEM)
    return pl.pallas_call(
        functools.partial(pack_kernel, tile_count, capacity),
        out_shape=[block] * tile_count,
        in_specs=[smem, smem, smem, vmem],
        out_specs=[vmem] * tile_count,
        scratch_shapes=[
            pltpu.SMEM((tile_count,), jnp.int32),
            pltpu.SMEM((tile_count * capacity,), jnp.int32),
        ],
        compiler_params=pltpu.CompilerParams(vmem_limit_bytes=56 * 2**20),
        name="pack_patterns",
    )(tile_ids, rows, cols, patterns)


def prepare_kernel(object_hbm, probe_ref, chirp_ref, field, lit, sems):
    rows, columns = object_hbm.shape[1:]
    modes, _, length, _ = probe_ref.shape
    loads = [
        pltpu.make_async_copy(
            object_hbm.at[:, :, tile * LANES : (tile + 1) * LANES],
            field.at[:, tile, 0:rows, :],
            sems.at[tile],
        )
        for tile in range(columns // LANES)
    ]
    for load in loads:
        load.start()
    for mode in range(modes):
        for band in range(length // BAND):
            at = pl.ds(band * BAND, BAND)
            cr, ci = chirp_ref[0, at, :], chirp_ref[1, at, :]
            pr, pi = probe_ref[mode, 0, at, :], probe_ref[mode, 1, at, :]
            lit[mode, 0, at, :] = cr * pr - ci * pi
            lit[mode, 1, at, :] = cr * pi + ci * pr
    for load in loads:
        load.wait()


def prepare(object_field, probe, chirp):
    _, rows, columns = object_field.shape
    vmem = pl.BlockSpec(memory_space=pltpu.VMEM)
    return pl.pallas_call(
        prepare_kernel,
        out_shape=[
            jax.ShapeDtypeStruct((2, columns // LANES + 1, rows + 8, LANES), jnp.float32),
            jax.ShapeDtypeStruct(probe.shape, jnp.float32),
        ],
        in_specs=[pl.BlockSpec(memory_space=pl.ANY), vmem, vmem],
        out_specs=[vmem, vmem],
        scratch_shapes=[pltpu.SemaphoreType.DMA((columns // LANES,))],
        compiler_params=pltpu.CompilerParams(vmem_limit_bytes=16 * 2**20),
        name="prepare_strip",
    )(object_field, probe, chirp)


def step_kernel(block_count, capacity, scale, first, last, field, lit, dft_ref, chirp_ref, *rest):
    blocks = rest[:block_count]
    rest = rest[block_count:]
    if not first:
        total_before, grad_before = rest[:2]
        rest = rest[2:]
    total, grad = rest[:2]
    rest = rest[2:]
    if last:
        quarters = rest[:SQUARE]
        rest = rest[SQUARE:]
    (
        pats,
        heads,
        corners,
        list_row,
        list_col,
        list_pat,
        patch_even,
        patch_odd,
        wide,
        tall,
        in_sem,
        out_sem,
    ) = rest
    modes, _, length, _ = lit.shape
    column_tiles, rows = total.shape[1:3]
    block_rows = capacity * length + HEAD
    bands = length // BAND

    loads = [
        pltpu.make_async_copy(
            blocks[b], pats.at[b * block_rows : (b + 1) * block_rows], in_sem.at[b]
        )
        for b in range(block_count)
    ]
    for load in loads:
        load.start()

    def begin(index, carry):
        at = pl.ds(pl.multiple_of(index * 8, 8), 8)
        for plane in range(2):
            for tile in range(column_tiles):
                total[plane, tile, at, :] = (
                    jnp.zeros((8, LANES), jnp.float32)
                    if first
                    else total_before[plane, tile, at, :]
                )
        return carry

    lax.fori_loop(0, rows // 8, begin, 0)
    grad[...] = jnp.zeros_like(grad) if first else grad_before[...]

    for load in loads:
        load.wait()
    for b in range(block_count):
        heads[b * HEAD : (b + 1) * HEAD, :] = (
            pats[(b + 1) * block_rows - HEAD : (b + 1) * block_rows, :]
            .astype(jnp.float32)
            .astype(jnp.int32)
        )
    fetch = pltpu.make_async_copy(heads, corners, in_sem.at[block_count])
    fetch.start()
    fetch.wait()

    number = jnp.int32(0)
    for b in range(block_count):

        def note(rank, at, b=b):
            first_line = b * HEAD
            list_row[at] = corners[first_line, rank] * DIGIT + corners[first_line + 1, rank]
            list_col[at] = corners[first_line + 2, rank] * DIGIT + corners[first_line + 3, rank]
            list_pat[at] = b * block_rows + rank * length
            return at + 1

        number = lax.fori_loop(0, corners[b * HEAD + 4, 0], note, number)

    patch = (patch_even, patch_odd)
    group = BAND
    span = 4
    groups = length // group
    tall_rows = modes * group

    def item(index):
        index = jnp.clip(index, 0, number - 1)
        row, col = list_row[index], list_col[index]
        shift = col % LANES
        return row, col // LANES, shift, pl.multiple_of(list_pat[index], LANES)

    def exit_chunks(index, side):
        row, col, shift, _ = item(index)
        slot = (index >> 1) & 1
        back = (LANES - shift) % LANES

        def chunk(band):
            at = pl.ds(band * BAND, BAND)
            at_field = pl.ds(row + band * BAND, BAND)
            lane = lax.broadcasted_iota(jnp.int32, (BAND, LANES), 1)
            planes = []
            for plane in range(2):
                left = pltpu.roll(field[plane, col, at_field, :], back, 1)
                right = pltpu.roll(field[plane, col + 1, at_field, :], back, 1)
                cell = jnp.where(lane < LANES - shift, left, right)
                cell = cell.astype(jnp.bfloat16).astype(jnp.float32)
                patch[side][slot, plane, at, :] = cell
                planes.append(cell)
            pr, pi = planes
            for mode in range(modes):
                lr, li = lit[mode, 0, at, :], lit[mode, 1, at, :]
                lanes = pl.ds(mode * length, length)
                wide[side, at, lanes] = (lr * pr - li * pi).astype(jnp.bfloat16)
                wide[side, pl.ds(length + band * BAND, BAND), lanes] = (
                    lr * pi + li * pr
                ).astype(jnp.bfloat16)

        return [functools.partial(chunk, band) for band in range(bands)]

    def column_chunks(source, target, table):
        def chunk(mode):
            both = min(2, modes - mode)
            out = jnp.dot(
                dft_ref[table],
                wide[source, :, mode * length : (mode + both) * length],
                preferred_element_type=jnp.float32,
            ).astype(jnp.bfloat16)
            for q in range(both):
                for g in range(groups):
                    at = pl.ds(g * tall_rows + (mode + q) * group, group)
                    for plane in range(2):
                        tall[target, at, plane * length : (plane + 1) * length] = out[
                            plane * length + g * group : plane * length + (g + 1) * group,
                            q * length : (q + 1) * length,
                        ]

        return [functools.partial(chunk, mode) for mode in range(0, modes, 2)]

    def row_product(source, table, g):
        out = jnp.dot(
            tall[source, g * tall_rows : (g + span) * tall_rows, :],
            dft_ref[table],
            preferred_element_type=jnp.float32,
        )
        return [
            [
                tuple(
                    out[
                        k * tall_rows + mode * group : k * tall_rows + (mode + 1) * group,
                        plane * length : (plane + 1) * length,
                    ]
                    for plane in range(2)
                )
                for mode in range(modes)
            ]
            for k in range(span)
        ]

    def far_chunks(index, side):
        _, _, _, source = item(index)
        weight = jnp.where((index >= 0) & (index < number), jnp.float32(1.0), jnp.float32(0.0))

        def chunk(g):
            for k, waves in enumerate(row_product(side, 1, g)):
                amplitude(g + k, waves)

        def amplitude(g, waves):
            bright = None
            for fr, fi in waves:
                power = fr * fr + fi * fi
                bright = power if bright is None else bright + power
            measured = pats[pl.ds(source + g * group, group), :].astype(jnp.float32)
            inverse = jnp.minimum(lax.rsqrt(bright), 1.0 / AMP_FLOOR)
            factor = (measured * inverse - 1.0) * weight
            for mode in range(modes):
                fr, fi = waves[mode]
                lanes = pl.ds(mode * length, length)
                wide[2, pl.ds(g * group, group), lanes] = (fr * factor).astype(jnp.bfloat16)
                wide[2, pl.ds(length + g * group, group), lanes] = (fi * factor).astype(
                    jnp.bfloat16
                )

        return [functools.partial(chunk, g) for g in range(0, groups, span)]

    def step_chunks(index, side):
        row, col, shift, _ = item(index)
        slot = (index >> 1) & 1

        def chunk(g):
            for k, waves in enumerate(row_product(2 + side, 0, g)):
                update(g + k, waves)

        def update(g, waves):
            at = pl.ds(g * group, group)
            at_field = pl.ds(row + g * group, group)
            lane = lax.broadcasted_iota(jnp.int32, (group, LANES), 1)
            pr, pi = patch[side][slot, 0, at, :], patch[side][slot, 1, at, :]
            steps = [None, None]
            for mode in range(modes):
                at_gr = pl.ds((2 * mode) * length + g * group, group)
                at_gi = pl.ds((2 * mode + 1) * length + g * group, group)
                lr, li = lit[mode, 0, at, :], lit[mode, 1, at, :]
                nr, ni = waves[mode]
                sr, si = lr * nr + li * ni, lr * ni - li * nr
                steps = [sr, si] if mode == 0 else [steps[0] + sr, steps[1] + si]
                grad[at_gr, :] += pr * nr + pi * ni
                grad[at_gi, :] += pr * ni - pi * nr
            places = [(plane, col + tile) for plane in range(2) for tile in range(2)]
            olds = [total[plane, tile, at_field, :] for plane, tile in places]
            sums = []
            for plane in range(2):
                moved = steps[plane].astype(jnp.bfloat16).astype(jnp.float32)
                moved = pltpu.roll(moved, shift, 1)
                sums.append(olds[2 * plane] + jnp.where(lane >= shift, moved, 0.0))
                sums.append(olds[2 * plane + 1] + jnp.where(lane < shift, moved, 0.0))
            for (plane, tile), value in zip(places, sums):
                total[plane, tile, at_field, :] = value

        return [functools.partial(chunk, g) for g in range(0, groups, span)]

    def run(*lists):
        order = []
        for rank, chunks in enumerate(lists):
            order += [((n + 0.5) / len(chunks), rank, chunk) for n, chunk in enumerate(chunks)]
        for _, _, chunk in sorted(order, key=lambda entry: entry[:2]):
            chunk()

    def visit(turn, carry):
        for side in range(2):
            at, other = 2 * turn + side, 1 - side
            run(far_chunks(at, side))
            run(column_chunks(other, other, 0), exit_chunks(at + 2, side))
            run(column_chunks(2, 2 + side, 1), step_chunks(at - 1, other))
        return carry

    @pl.when(number > 0)
    def _():
        tall[3] = jnp.zeros(tall.shape[1:], tall.dtype)
        patch[1][1] = jnp.zeros(patch[1].shape[1:], jnp.float32)
        run(exit_chunks(jnp.int32(0), 0))
        run(column_chunks(0, 0, 0), exit_chunks(jnp.int32(1), 1))
        lax.fori_loop(0, (number + 1) // 2, visit, 0)

        @pl.when(number % 2 == 0)
        def _():
            run(step_chunks(number - 1, 1))

    if not last:
        return
    for mode in range(modes):
        for band in range(bands):
            at = pl.ds(band * BAND, BAND)
            at_gr = pl.ds((2 * mode) * length + band * BAND, BAND)
            at_gi = pl.ds((2 * mode + 1) * length + band * BAND, BAND)
            cr, ci = chirp_ref[0, at, :] * scale, chirp_ref[1, at, :] * scale
            gr, gi = grad[at_gr, :], grad[at_gi, :]
            grad[at_gr, :] = cr * gr + ci * gi
            grad[at_gi, :] = cr * gi - ci * gr
    pos = lax.axis_index("pos")
    me = lax.axis_index("tile") % (SQUARE // 2) * 2 + pos
    quarter = grad.shape[0] // SQUARE
    parts = [
        (grad.at[pl.ds(pl.multiple_of((me ^ turn) * quarter, 8), quarter), :], outside)
        for turn, outside in enumerate(quarters)
    ]
    stores = [
        pltpu.make_async_copy(inside, outside, out_sem.at[n])
        for n, (inside, outside) in enumerate(parts)
    ]
    for store in stores:
        store.start()
    for store in stores:
        store.wait()


def step(field, lit, blocks, tables, scale, capacity, before, last):
    modes, _, length, _ = lit.shape
    column_tiles, rows = field.shape[1:3]
    count = len(blocks)
    slots = count * capacity
    vmem = pl.BlockSpec(memory_space=pltpu.VMEM)
    hbm = pl.BlockSpec(memory_space=pl.ANY)
    f32, bf16 = jnp.float32, jnp.bfloat16
    outs = [
        jax.ShapeDtypeStruct(field.shape, f32),
        jax.ShapeDtypeStruct((2 * modes * length, length), f32),
    ]
    specs = [vmem, vmem]
    if last:
        outs += [jax.ShapeDtypeStruct((2 * modes * length // SQUARE, length), f32)] * SQUARE
        specs += [hbm] * SQUARE
    return pl.pallas_call(
        functools.partial(step_kernel, count, capacity, scale, not before, last),
        out_shape=outs,
        in_specs=[vmem] * 4 + [hbm] * count + [vmem] * len(before),
        out_specs=specs,
        scratch_shapes=[
            pltpu.VMEM((count * (capacity * length + HEAD), length), bf16),
            pltpu.VMEM((count * HEAD, LANES), jnp.int32),
            pltpu.SMEM((count * HEAD, LANES), jnp.int32),
            pltpu.SMEM((slots,), jnp.int32),
            pltpu.SMEM((slots,), jnp.int32),
            pltpu.SMEM((slots,), jnp.int32),
            pltpu.VMEM((2, 2, length, length), f32),
            pltpu.VMEM((2, 2, length, length), f32),
            pltpu.VMEM((3, 2 * length, modes * length), bf16),
            pltpu.VMEM((4, modes * length, 2 * length), bf16),
            pltpu.SemaphoreType.DMA((count + 1,)),
            pltpu.SemaphoreType.DMA((SQUARE,)),
        ],
        compiler_params=pltpu.CompilerParams(vmem_limit_bytes=26 * 2**20),
        cost_estimate=pl.CostEstimate(
            flops=slots * modes * 4 * 8 * length**3,
            bytes_accessed=16 * 2**20,
            transcendentals=slots * length**2,
        ),
        name="gradient_step",
    )(field, lit, *tables, *blocks, *before)


def give_kernel(total, send, sems):
    half = send.shape[2] // LANES
    side = 1 - lax.axis_index("pos")
    stores = [
        pltpu.make_async_copy(
            total.at[:, side * half + tile, 0 : send.shape[1], :],
            send.at[:, :, tile * LANES : (tile + 1) * LANES],
            sems.at[tile],
        )
        for tile in range(half)
    ]
    for store in stores:
        store.start()
    for store in stores:
        store.wait()


def finish_kernel(total, received, out):
    half = out.shape[2] // LANES
    side = lax.axis_index("pos")

    def add(index, carry):
        at = pl.ds(pl.multiple_of(index * 8, 8), 8)
        for plane in range(2):
            for tile in range(half):
                lanes = pl.ds(tile * LANES, LANES)
                out[plane, at, lanes] = (
                    total[plane, side * half + tile, at, :] + received[plane, at, lanes]
                )
        return carry

    lax.fori_loop(0, out.shape[1] // 8, add, 0)


def halves(total, received=None):
    _, column_tiles, rows, _ = total.shape
    half = (column_tiles - 1) // 2
    shape = jax.ShapeDtypeStruct((2, rows - 8, half * LANES), jnp.float32)
    vmem = pl.BlockSpec(memory_space=pltpu.VMEM)
    cost = pl.CostEstimate(flops=2**20, bytes_accessed=4 * 2**20, transcendentals=0)
    limit = pltpu.CompilerParams(vmem_limit_bytes=16 * 2**20)
    if received is None:
        return pl.pallas_call(
            give_kernel,
            out_shape=shape,
            in_specs=[vmem],
            out_specs=pl.BlockSpec(memory_space=pl.ANY),
            scratch_shapes=[pltpu.SemaphoreType.DMA((half,))],
            compiler_params=limit,
            cost_estimate=cost,
            name="give_half",
        )(total)
    return pl.pallas_call(
        finish_kernel,
        out_shape=shape,
        in_specs=[vmem, vmem],
        out_specs=vmem,
        compiler_params=limit,
        cost_estimate=cost,
        name="add_half",
    )(total, received)


def from_peer(array, turn, devices):
    pairs = [(i, i ^ turn) for i in range(devices)]
    return lax.ppermute(array, ("tile", "pos"), pairs)


def tree_sum(parts):
    while len(parts) > 1:
        parts = [a + b for a, b in zip(parts[::2], parts[1::2])]
    return parts[0]


def on_device(object_field, probe, patterns, scan_tile, scan_row, scan_col):
    tile_count = lax.axis_size("tile")
    pos_count = lax.axis_size("pos")
    number, length = patterns.shape[0], patterns.shape[-1]
    capacity = max(2, 2 * number // tile_count)
    scale = 1.0 / math.sqrt(number * tile_count * pos_count)
    tables = (jnp.asarray(dft_tables(length)), jnp.asarray(chirp_table(length)))
    blocks = pack(patterns, scan_tile[:, 0], scan_row, scan_col, tile_count, capacity)
    field, lit = prepare(object_field, probe, tables[1])
    late = tile_count * 3 // 4
    order = [*range(late - tile_count // 4), *range(late, tile_count), *range(tile_count // 2, late)]
    arrived = [blocks[0]]
    for hop in order[1:]:
        block = blocks[hop]
        if len(arrived) >= late:
            block = lax.optimization_barrier((block, arrived[1], lit))[0]
        arrived.append(lax.ppermute(block, "tile", [(i, i ^ hop) for i in range(tile_count)]))
    cuts = [0, tile_count // 2, tile_count * 3 // 4, tile_count]
    sums = ()
    for a, b in zip(cuts[:-1], cuts[1:]):
        sums = step(field, lit, arrived[a:b], tables, scale, capacity, sums, b == tile_count)
    total, grads = sums[0], sums[2:]

    devices = tile_count * pos_count
    inside, across = range(1, SQUARE), range(SQUARE, devices, SQUARE)
    part = tree_sum([grads[0]] + [from_peer(grads[turn], turn, devices) for turn in inside])
    send, part = lax.optimization_barrier((halves(total), part))
    object_step = halves(total, lax.ppermute(send, "pos", [(0, 1), (1, 0)]))
    part = part.astype(jnp.bfloat16)
    received = [from_peer(part, turn, devices) for turn in across]
    object_step, *received = lax.optimization_barrier([object_step] + received)
    part = tree_sum([piece.astype(jnp.float32) for piece in [part] + received])
    square = [part] + [from_peer(part, turn, devices) for turn in inside]
    me = lax.axis_index(("tile", "pos"))
    for bit in (1, 2):
        swapped = (me & bit) != 0
        square = [jnp.where(swapped, square[q ^ bit], square[q]) for q in range(SQUARE)]
    return (object_step, jnp.concatenate(square).reshape(probe.shape))


def solution(mesh):
    placed = (
        P("groups", "tile", None),
        P("groups", None, None, None),
        P(("groups", "tile", "pos"), None, None),
        P(("groups", "tile", "pos"), None),
        P(("groups", "tile", "pos")),
        P(("groups", "tile", "pos")),
    )
    return jax.shard_map(
        on_device,
        mesh=mesh,
        in_specs=placed,
        out_specs=(P("groups", "tile", "pos"), P("groups", None, None, None)),
        check_vma=False,
    )
```

```python
import functools
import math

import jax
import jax.numpy as jnp
import numpy as np
from jax import lax
from jax.experimental import pallas as pl
from jax.experimental.pallas import tpu as pltpu
from jax.sharding import PartitionSpec as P

AMP_FLOOR = 0.5
HEAD = 16
DIGIT = 16
LANES = 128
SQUARE = 4

BAND = 16


def dft_tables(length):
    indices = np.arange(length, dtype=np.int32)
    products = indices[:, None] * indices[None, :] % length
    angles = products.astype(np.float32) * np.float32(-2.0 * math.pi / length)
    factor = np.float32(1.0 / math.sqrt(length))
    real = (np.cos(angles) * factor).astype(jnp.bfloat16)
    imag = (np.sin(angles) * factor).astype(jnp.bfloat16)
    forward = np.block([[real, -imag], [imag, real]])
    backward = np.block([[real, imag], [-imag, real]])
    return np.stack([forward, backward])


def chirp_table(length):
    offsets = np.arange(length, dtype=np.int32) - length // 2
    squares = offsets * offsets
    phases = (squares[:, None] + squares[None, :]).astype(np.float32) * np.float32(
        0.5 * math.pi / length
    )
    return np.stack([np.cos(phases), np.sin(phases)]).astype(np.float32)


def pack_kernel(tile_count, capacity, tile_ref, row_ref, col_ref, pat_ref, *rest):
    blocks, count_ref, source_ref = rest[:tile_count], rest[tile_count], rest[tile_count + 1]
    number, length = pat_ref.shape[0], pat_ref.shape[1]
    me = lax.axis_index("tile")
    for hop in range(tile_count):
        count_ref[hop] = 0

    def place(index, carry):
        hop = tile_ref[index] ^ me
        rank = count_ref[hop]
        count_ref[hop] = rank + 1
        source_ref[hop * capacity + rank] = index
        return carry

    lax.fori_loop(0, number, place, 0)
    lane = lax.broadcasted_iota(jnp.int32, (HEAD, LANES), 1)
    line = lax.broadcasted_iota(jnp.int32, (HEAD, LANES), 0)
    for hop in range(tile_count):
        count = count_ref[hop]
        corner = jnp.zeros((HEAD, LANES), jnp.int32)
        for rank in range(capacity):
            valid = rank < count
            index = jnp.where(valid, source_ref[hop * capacity + rank], 0)
            value = jnp.where(line < 2, row_ref[index], col_ref[index])
            corner = jnp.where((lane == rank) & valid, value, corner)

            @pl.when(valid)
            def _(hop=hop, rank=rank, index=index):
                blocks[hop][rank * length : (rank + 1) * length, :] = pat_ref[index]

        digits = jnp.where(line % 2 == 0, corner // DIGIT, corner % DIGIT)
        digits = jnp.where(line < 4, digits, jnp.where(line == 4, count, 0))
        blocks[hop][capacity * length :, :] = digits.astype(jnp.float32).astype(jnp.bfloat16)


def pack(patterns, tile_ids, rows, cols, tile_count, capacity):
    length = patterns.shape[-1]
    block = jax.ShapeDtypeStruct((capacity * length + HEAD, length), jnp.bfloat16)
    smem = pl.BlockSpec(memory_space=pltpu.SMEM)
    vmem = pl.BlockSpec(memory_space=pltpu.VMEM)
    return pl.pallas_call(
        functools.partial(pack_kernel, tile_count, capacity),
        out_shape=[block] * tile_count,
        in_specs=[smem, smem, smem, vmem],
        out_specs=[vmem] * tile_count,
        scratch_shapes=[
            pltpu.SMEM((tile_count,), jnp.int32),
            pltpu.SMEM((tile_count * capacity,), jnp.int32),
        ],
        compiler_params=pltpu.CompilerParams(vmem_limit_bytes=56 * 2**20),
        name="pack_patterns",
    )(tile_ids, rows, cols, patterns)


def prepare_kernel(object_hbm, probe_ref, chirp_ref, field, lit, sems):
    rows, columns = object_hbm.shape[1:]
    modes, _, length, _ = probe_ref.shape
    loads = [
        pltpu.make_async_copy(
            object_hbm.at[:, :, tile * LANES : (tile + 1) * LANES],
            field.at[:, tile, 0:rows, :],
            sems.at[tile],
        )
        for tile in range(columns // LANES)
    ]
    for load in loads:
        load.start()
    for mode in range(modes):
        for band in range(length // BAND):
            at = pl.ds(band * BAND, BAND)
            cr, ci = chirp_ref[0, at, :], chirp_ref[1, at, :]
            pr, pi = probe_ref[mode, 0, at, :], probe_ref[mode, 1, at, :]
            lit[mode, 0, at, :] = cr * pr - ci * pi
            lit[mode, 1, at, :] = cr * pi + ci * pr
    for load in loads:
        load.wait()


def prepare(object_field, probe, chirp):
    _, rows, columns = object_field.shape
    vmem = pl.BlockSpec(memory_space=pltpu.VMEM)
    return pl.pallas_call(
        prepare_kernel,
        out_shape=[
            jax.ShapeDtypeStruct((2, columns // LANES + 1, rows + 8, LANES), jnp.float32),
            jax.ShapeDtypeStruct(probe.shape, jnp.float32),
        ],
        in_specs=[pl.BlockSpec(memory_space=pl.ANY), vmem, vmem],
        out_specs=[vmem, vmem],
        scratch_shapes=[pltpu.SemaphoreType.DMA((columns // LANES,))],
        compiler_params=pltpu.CompilerParams(vmem_limit_bytes=16 * 2**20),
        name="prepare_strip",
    )(object_field, probe, chirp)


def step_kernel(block_count, capacity, scale, first, last, field, lit, dft_ref, chirp_ref, *rest):
    blocks = rest[:block_count]
    rest = rest[block_count:]
    if not first:
        total_before, grad_before = rest[:2]
        rest = rest[2:]
    total, grad = rest[:2]
    rest = rest[2:]
    if last:
        quarters = rest[:SQUARE]
        rest = rest[SQUARE:]
    (
        pats,
        heads,
        corners,
        list_row,
        list_col,
        list_pat,
        patch_even,
        patch_odd,
        wide,
        tall,
        in_sem,
        out_sem,
    ) = rest
    modes, _, length, _ = lit.shape
    column_tiles, rows = total.shape[1:3]
    block_rows = capacity * length + HEAD
    bands = length // BAND

    loads = [
        pltpu.make_async_copy(
            blocks[b], pats.at[b * block_rows : (b + 1) * block_rows], in_sem.at[b]
        )
        for b in range(block_count)
    ]
    for load in loads:
        load.start()

    def begin(index, carry):
        at = pl.ds(pl.multiple_of(index * 8, 8), 8)
        for plane in range(2):
            for tile in range(column_tiles):
                total[plane, tile, at, :] = (
                    jnp.zeros((8, LANES), jnp.float32)
                    if first
                    else total_before[plane, tile, at, :]
                )
        return carry

    lax.fori_loop(0, rows // 8, begin, 0)
    grad[...] = jnp.zeros_like(grad) if first else grad_before[...]

    for load in loads:
        load.wait()
    for b in range(block_count):
        heads[b * HEAD : (b + 1) * HEAD, :] = (
            pats[(b + 1) * block_rows - HEAD : (b + 1) * block_rows, :]
            .astype(jnp.float32)
            .astype(jnp.int32)
        )
    fetch = pltpu.make_async_copy(heads, corners, in_sem.at[block_count])
    fetch.start()
    fetch.wait()

    number = jnp.int32(0)
    for b in range(block_count):

        def note(rank, at, b=b):
            first_line = b * HEAD
            list_row[at] = corners[first_line, rank] * DIGIT + corners[first_line + 1, rank]
            list_col[at] = corners[first_line + 2, rank] * DIGIT + corners[first_line + 3, rank]
            list_pat[at] = b * block_rows + rank * length
            return at + 1

        number = lax.fori_loop(0, corners[b * HEAD + 4, 0], note, number)

    patch = (patch_even, patch_odd)
    group = BAND
    span = 4
    groups = length // group
    tall_rows = modes * group

    def item(index):
        index = jnp.clip(index, 0, number - 1)
        row, col = list_row[index], list_col[index]
        shift = col % LANES
        return row, col // LANES, shift, pl.multiple_of(list_pat[index], LANES)

    def exit_chunks(index, side):
        row, col, shift, _ = item(index)
        slot = (index >> 1) & 1
        back = (LANES - shift) % LANES

        def chunk(band):
            at = pl.ds(band * BAND, BAND)
            at_field = pl.ds(row + band * BAND, BAND)
            lane = lax.broadcasted_iota(jnp.int32, (BAND, LANES), 1)
            planes = []
            for plane in range(2):
                left = pltpu.roll(field[plane, col, at_field, :], back, 1)
                right = pltpu.roll(field[plane, col + 1, at_field, :], back, 1)
                cell = jnp.where(lane < LANES - shift, left, right)
                cell = cell.astype(jnp.bfloat16).astype(jnp.float32)
                patch[side][slot, plane, at, :] = cell
                planes.append(cell)
            pr, pi = planes
            for mode in range(modes):
                lr, li = lit[mode, 0, at, :], lit[mode, 1, at, :]
                lanes = pl.ds(mode * length, length)
                wide[side, at, lanes] = (lr * pr - li * pi).astype(jnp.bfloat16)
                wide[side, pl.ds(length + band * BAND, BAND), lanes] = (
                    lr * pi + li * pr
                ).astype(jnp.bfloat16)

        return [functools.partial(chunk, band) for band in range(bands)]

    def column_chunks(source, target, table):
        def chunk(mode):
            both = min(2, modes - mode)
            out = jnp.dot(
                dft_ref[table],
                wide[source, :, mode * length : (mode + both) * length],
                preferred_element_type=jnp.float32,
            ).astype(jnp.bfloat16)
            for q in range(both):
                for g in range(groups):
                    at = pl.ds(g * tall_rows + (mode + q) * group, group)
                    for plane in range(2):
                        tall[target, at, plane * length : (plane + 1) * length] = out[
                            plane * length + g * group : plane * length + (g + 1) * group,
                            q * length : (q + 1) * length,
                        ]

        return [functools.partial(chunk, mode) for mode in range(0, modes, 2)]

    def row_product(source, table, g):
        out = jnp.dot(
            tall[source, g * tall_rows : (g + span) * tall_rows, :],
            dft_ref[table],
            preferred_element_type=jnp.float32,
        )
        return [
            [
                tuple(
                    out[
                        k * tall_rows + mode * group : k * tall_rows + (mode + 1) * group,
                        plane * length : (plane + 1) * length,
                    ]
                    for plane in range(2)
                )
                for mode in range(modes)
            ]
            for k in range(span)
        ]

    def far_chunks(index, side):
        _, _, _, source = item(index)
        weight = jnp.where((index >= 0) & (index < number), jnp.float32(1.0), jnp.float32(0.0))

        def chunk(g):
            for k, waves in enumerate(row_product(side, 1, g)):
                amplitude(g + k, waves)

        def amplitude(g, waves):
            bright = None
            for fr, fi in waves:
                power = fr * fr + fi * fi
                bright = power if bright is None else bright + power
            measured = pats[pl.ds(source + g * group, group), :].astype(jnp.float32)
            inverse = jnp.minimum(lax.rsqrt(bright), 1.0 / AMP_FLOOR)
            factor = (measured * inverse - 1.0) * weight
            for mode in range(modes):
                fr, fi = waves[mode]
                lanes = pl.ds(mode * length, length)
                wide[2, pl.ds(g * group, group), lanes] = (fr * factor).astype(jnp.bfloat16)
                wide[2, pl.ds(length + g * group, group), lanes] = (fi * factor).astype(
                    jnp.bfloat16
                )

        return [functools.partial(chunk, g) for g in range(0, groups, span)]

    def step_chunks(index, side):
        row, col, shift, _ = item(index)
        slot = (index >> 1) & 1

        def chunk(g):
            for k, waves in enumerate(row_product(2 + side, 0, g)):
                update(g + k, waves)

        def update(g, waves):
            at = pl.ds(g * group, group)
            at_field = pl.ds(row + g * group, group)
            lane = lax.broadcasted_iota(jnp.int32, (group, LANES), 1)
            pr, pi = patch[side][slot, 0, at, :], patch[side][slot, 1, at, :]
            steps = [None, None]
            for mode in range(modes):
                at_gr = pl.ds((2 * mode) * length + g * group, group)
                at_gi = pl.ds((2 * mode + 1) * length + g * group, group)
                lr, li = lit[mode, 0, at, :], lit[mode, 1, at, :]
                nr, ni = waves[mode]
                sr, si = lr * nr + li * ni, lr * ni - li * nr
                steps = [sr, si] if mode == 0 else [steps[0] + sr, steps[1] + si]
                grad[at_gr, :] += pr * nr + pi * ni
                grad[at_gi, :] += pr * ni - pi * nr
            places = [(plane, col + tile) for plane in range(2) for tile in range(2)]
            olds = [total[plane, tile, at_field, :] for plane, tile in places]
            sums = []
            for plane in range(2):
                moved = steps[plane].astype(jnp.bfloat16).astype(jnp.float32)
                moved = pltpu.roll(moved, shift, 1)
                sums.append(olds[2 * plane] + jnp.where(lane >= shift, moved, 0.0))
                sums.append(olds[2 * plane + 1] + jnp.where(lane < shift, moved, 0.0))
            for (plane, tile), value in zip(places, sums):
                total[plane, tile, at_field, :] = value

        return [functools.partial(chunk, g) for g in range(0, groups, span)]

    def run(*lists):
        order = []
        for rank, chunks in enumerate(lists):
            order += [((n + 0.5) / len(chunks), rank, chunk) for n, chunk in enumerate(chunks)]
        for _, _, chunk in sorted(order, key=lambda entry: entry[:2]):
            chunk()

    def visit(turn, carry):
        for side in range(2):
            at, other = 2 * turn + side, 1 - side
            run(far_chunks(at, side))
            run(column_chunks(other, other, 0), exit_chunks(at + 2, side))
            run(column_chunks(2, 2 + side, 1), step_chunks(at - 1, other))
        return carry

    @pl.when(number > 0)
    def _():
        tall[3] = jnp.zeros(tall.shape[1:], tall.dtype)
        patch[1][1] = jnp.zeros(patch[1].shape[1:], jnp.float32)
        run(exit_chunks(jnp.int32(0), 0))
        run(column_chunks(0, 0, 0), exit_chunks(jnp.int32(1), 1))
        lax.fori_loop(0, (number + 1) // 2, visit, 0)

        @pl.when(number % 2 == 0)
        def _():
            run(step_chunks(number - 1, 1))

    if not last:
        return
    for mode in range(modes):
        for band in range(bands):
            at = pl.ds(band * BAND, BAND)
            at_gr = pl.ds((2 * mode) * length + band * BAND, BAND)
            at_gi = pl.ds((2 * mode + 1) * length + band * BAND, BAND)
            cr, ci = chirp_ref[0, at, :] * scale, chirp_ref[1, at, :] * scale
            gr, gi = grad[at_gr, :], grad[at_gi, :]
            grad[at_gr, :] = cr * gr + ci * gi
            grad[at_gi, :] = cr * gi - ci * gr
    pos = lax.axis_index("pos")
    me = lax.axis_index("tile") % (SQUARE // 2) * 2 + pos
    quarter = grad.shape[0] // SQUARE
    parts = [
        (grad.at[pl.ds(pl.multiple_of((me ^ turn) * quarter, 8), quarter), :], outside)
        for turn, outside in enumerate(quarters)
    ]
    stores = [
        pltpu.make_async_copy(inside, outside, out_sem.at[n])
        for n, (inside, outside) in enumerate(parts)
    ]
    for store in stores:
        store.start()
    for store in stores:
        store.wait()


def step(field, lit, blocks, tables, scale, capacity, before, last):
    modes, _, length, _ = lit.shape
    column_tiles, rows = field.shape[1:3]
    count = len(blocks)
    slots = count * capacity
    vmem = pl.BlockSpec(memory_space=pltpu.VMEM)
    hbm = pl.BlockSpec(memory_space=pl.ANY)
    f32, bf16 = jnp.float32, jnp.bfloat16
    outs = [
        jax.ShapeDtypeStruct(field.shape, f32),
        jax.ShapeDtypeStruct((2 * modes * length, length), f32),
    ]
    specs = [vmem, vmem]
    if last:
        outs += [jax.ShapeDtypeStruct((2 * modes * length // SQUARE, length), f32)] * SQUARE
        specs += [hbm] * SQUARE
    return pl.pallas_call(
        functools.partial(step_kernel, count, capacity, scale, not before, last),
        out_shape=outs,
        in_specs=[vmem] * 4 + [hbm] * count + [vmem] * len(before),
        out_specs=specs,
        scratch_shapes=[
            pltpu.VMEM((count * (capacity * length + HEAD), length), bf16),
            pltpu.VMEM((count * HEAD, LANES), jnp.int32),
            pltpu.SMEM((count * HEAD, LANES), jnp.int32),
            pltpu.SMEM((slots,), jnp.int32),
            pltpu.SMEM((slots,), jnp.int32),
            pltpu.SMEM((slots,), jnp.int32),
            pltpu.VMEM((2, 2, length, length), f32),
            pltpu.VMEM((2, 2, length, length), f32),
            pltpu.VMEM((3, 2 * length, modes * length), bf16),
            pltpu.VMEM((4, modes * length, 2 * length), bf16),
            pltpu.SemaphoreType.DMA((count + 1,)),
            pltpu.SemaphoreType.DMA((SQUARE,)),
        ],
        compiler_params=pltpu.CompilerParams(vmem_limit_bytes=26 * 2**20),
        cost_estimate=pl.CostEstimate(
            flops=slots * modes * 4 * 8 * length**3,
            bytes_accessed=16 * 2**20,
            transcendentals=slots * length**2,
        ),
        name="gradient_step",
    )(field, lit, *tables, *blocks, *before)


def give_kernel(total, send, sems):
    half = send.shape[2] // LANES
    side = 1 - lax.axis_index("pos")
    stores = [
        pltpu.make_async_copy(
            total.at[:, side * half + tile, 0 : send.shape[1], :],
            send.at[:, :, tile * LANES : (tile + 1) * LANES],
            sems.at[tile],
        )
        for tile in range(half)
    ]
    for store in stores:
        store.start()
    for store in stores:
        store.wait()


def finish_kernel(total, received, out):
    half = out.shape[2] // LANES
    side = lax.axis_index("pos")

    def add(index, carry):
        at = pl.ds(pl.multiple_of(index * 8, 8), 8)
        for plane in range(2):
            for tile in range(half):
                lanes = pl.ds(tile * LANES, LANES)
                out[plane, at, lanes] = (
                    total[plane, side * half + tile, at, :] + received[plane, at, lanes]
                )
        return carry

    lax.fori_loop(0, out.shape[1] // 8, add, 0)


def halves(total, received=None):
    _, column_tiles, rows, _ = total.shape
    half = (column_tiles - 1) // 2
    shape = jax.ShapeDtypeStruct((2, rows - 8, half * LANES), jnp.float32)
    vmem = pl.BlockSpec(memory_space=pltpu.VMEM)
    cost = pl.CostEstimate(flops=2**20, bytes_accessed=4 * 2**20, transcendentals=0)
    limit = pltpu.CompilerParams(vmem_limit_bytes=16 * 2**20)
    if received is None:
        return pl.pallas_call(
            give_kernel,
            out_shape=shape,
            in_specs=[vmem],
            out_specs=pl.BlockSpec(memory_space=pl.ANY),
            scratch_shapes=[pltpu.SemaphoreType.DMA((half,))],
            compiler_params=limit,
            cost_estimate=cost,
            name="give_half",
        )(total)
    return pl.pallas_call(
        finish_kernel,
        out_shape=shape,
        in_specs=[vmem, vmem],
        out_specs=vmem,
        compiler_params=limit,
        cost_estimate=cost,
        name="add_half",
    )(total, received)


def from_peer(array, turn, devices):
    pairs = [(i, i ^ turn) for i in range(devices)]
    return lax.ppermute(array, ("tile", "pos"), pairs)


def tree_sum(parts):
    while len(parts) > 1:
        parts = [a + b for a, b in zip(parts[::2], parts[1::2])]
    return parts[0]


def on_device(object_field, probe, patterns, scan_tile, scan_row, scan_col):
    tile_count = lax.axis_size("tile")
    pos_count = lax.axis_size("pos")
    number, length = patterns.shape[0], patterns.shape[-1]
    capacity = max(2, 2 * number // tile_count)
    scale = 1.0 / math.sqrt(number * tile_count * pos_count)
    tables = (jnp.asarray(dft_tables(length)), jnp.asarray(chirp_table(length)))
    blocks = pack(patterns, scan_tile[:, 0], scan_row, scan_col, tile_count, capacity)
    field, lit = prepare(object_field, probe, tables[1])
    late = tile_count * 3 // 4
    order = [*range(late - tile_count // 4), *range(late, tile_count), *range(tile_count // 2, late)]
    arrived = [blocks[0]]
    for hop in order[1:]:
        block = blocks[hop]
        if len(arrived) >= late:
            block = lax.optimization_barrier((block, arrived[1], lit))[0]
        arrived.append(lax.ppermute(block, "tile", [(i, i ^ hop) for i in range(tile_count)]))
    cuts = [0, tile_count // 2, tile_count * 3 // 4, tile_count]
    sums = ()
    for a, b in zip(cuts[:-1], cuts[1:]):
        sums = step(field, lit, arrived[a:b], tables, scale, capacity, sums, b == tile_count)
    total, grads = sums[0], sums[2:]

    devices = tile_count * pos_count
    across = range(SQUARE, devices, SQUARE)
    near = grads[0] + from_peer(grads[1], 1, devices)
    part = near + from_peer(grads[2] + from_peer(grads[3], 1, devices), 2, devices)
    send, part = lax.optimization_barrier((halves(total), part))
    object_step = halves(total, lax.ppermute(send, "pos", [(0, 1), (1, 0)]))
    part = part.astype(jnp.bfloat16)
    received = [from_peer(part, turn, devices) for turn in across]
    object_step, *received = lax.optimization_barrier([object_step] + received)
    part = tree_sum([piece.astype(jnp.float32) for piece in [part] + received])
    square = [part, from_peer(part, 1, devices)]
    square += [from_peer(part, 2, devices)]
    square += [from_peer(square[2], 1, devices)]
    me = lax.axis_index(("tile", "pos"))
    for bit in (1, 2):
        swapped = (me & bit) != 0
        square = [jnp.where(swapped, square[q ^ bit], square[q]) for q in range(SQUARE)]
    return (object_step, jnp.concatenate(square).reshape(probe.shape))


def solution(mesh):
    placed = (
        P("groups", "tile", None),
        P("groups", None, None, None),
        P(("groups", "tile", "pos"), None, None),
        P(("groups", "tile", "pos"), None),
        P(("groups", "tile", "pos")),
        P(("groups", "tile", "pos")),
    )
    return jax.shard_map(
        on_device,
        mesh=mesh,
        in_specs=placed,
        out_specs=(P("groups", "tile", "pos"), P("groups", None, None, None)),
        check_vma=False,
    )
```
